256 devices in a mesh: ctx: 16 (over z, y_lo), head: 8 (over x, y_hi), dp: 2 (over core).
Axes of the slice: x: 4, y: 4 (y_hi: 2, y_lo: 2; y = y_hi * 2 + y_lo), z: 8, core: 2. Of those that a mesh axis runs over, the one named last changes fastest.
Arguments:
- queries: bfloat16 [24576, 5120], P(('dp', 'ctx'), 'head'), parts along dimension 0, may hold values from -60 to 60
- query_tangent: bfloat16 [24576, 5120], P(('dp', 'ctx'), 'head'), parts along dimension 0, may hold values from -6 to 6
- keys: bfloat16 [4096, 5120], P(('dp', 'ctx'), 'head'), parts along dimension 0, may hold values from -60 to 60
- key_tangent: bfloat16 [4096, 5120], P(('dp', 'ctx'), 'head'), parts along dimension 0, may hold values from -6 to 6
- values: bfloat16 [4096, 5120], P(('dp', 'ctx'), 'head'), parts along dimension 0, may hold values from -6 to 6
- value_tangent: bfloat16 [4096, 5120], P(('dp', 'ctx'), 'head'), parts along dimension 0, may hold values from -6 to 6
- query_gain: float32 [5120], P('head'), may hold values from 0.8 to 2.5
- key_gain: float32 [5120], P('head'), may hold values from 0.8 to 2.5
Outputs:
- attended: bfloat16 [24576, 5120], P(('dp', 'ctx'), 'head'), parts along dimension 0
- attended_tangent: bfloat16 [24576, 5120], P(('dp', 'ctx'), 'head'), parts along dimension 0
The draws below stay inside these ranges and needn't reach their ends.
There are 2 independent parts, one for each index of `dp`. The reference program is written for one: setup_inputs(seed, part) draws one part's arguments, and reference() takes and returns one part's arrays. A program takes and returns all parts, laid end to end along the dimension named above; an argument that names none is the same for every part. Nothing has to cross between parts.
All inputs are finite; a program needn't handle non-finite values.
Results may differ from the reference program's by a relative error of at most 0.012.
The reference program's roundings to bfloat16 on the way count: a program that leaves them out, or rounds other values in their place, can miss the bound.
Values may be sent and summed in bfloat16 or wider, within the bound.
A program may use at most 128 MiB of HBM per device.

```python
import math
import jax
import jax.numpy as jnp
from jax import lax

D = 5120
HEADS = 40
HEAD_DIM = 128
QTOK = 12288
KEYS = 2048


def shared_base(key):
    return jax.random.normal(key, (KEYS, D), jnp.float32)


def column_scale(top):
    return jnp.exp(jnp.log(top) * jnp.arange(D, dtype=jnp.float32) / D)


def draw_keys(key, part):
    base = shared_base(key)
    field = base * column_scale(3.0)
    return jnp.clip(field, -60.0, 60.0).astype(jnp.bfloat16)


def draw_queries(key, part):
    key = jax.random.fold_in(key, 23)
    fresh = jax.random.normal(key, (QTOK, D), jnp.float32)
    field = fresh * column_scale(3.0)
    return jnp.clip(field, -60.0, 60.0).astype(jnp.bfloat16)


def levels(rng, dims, split, least, largest):
    level, own = 1.0, jax.random.fold_in(rng, 6)
    for position, shards_of in split:
        heights = jnp.exp(jax.random.uniform(jax.random.fold_in(own, position), (shards_of,), jnp.float32, least / len(split), largest / len(split)))
        level = level * jnp.repeat(heights, dims[position] // shards_of).reshape([-1 if axis == position else 1 for axis in range(len(dims))])
    return level


def gaussian(key, dims, scale, limit, split=(), kind=jnp.bfloat16):
    level = levels(key, dims, split, -0.22, 0.18) if split else 1.0
    entries = jax.random.normal(key, dims, jnp.float32) * scale * level
    return jnp.minimum(jnp.maximum(entries, -limit), limit).astype(kind)


def setup_inputs(seed: int = 0, part: int = 0) -> dict:
    seeds = jax.random.split(jax.random.key(seed), 9)
    own_keys = jax.random.split(jax.random.fold_in(seeds[8], part), 9)
    return {
        "queries": draw_queries(jax.random.fold_in(jax.random.fold_in(seeds[8], part), 71), part),
        "query_tangent": gaussian(own_keys[1], (QTOK, D), 1.0, 6.0, ((0, 16), (1, 8))),
        "keys": draw_keys(jax.random.fold_in(jax.random.fold_in(seeds[8], part), 71), part),
        "key_tangent": gaussian(own_keys[3], (KEYS, D), 1.0, 6.0, ((0, 16), (1, 8))),
        "values": gaussian(own_keys[4], (KEYS, D), 1.0, 6.0, ((0, 16), (1, 8))),
        "value_tangent": gaussian(own_keys[5], (KEYS, D), 1.0, 6.0, ((0, 16), (1, 8))),
        "query_gain": jnp.clip(jnp.exp(math.log(2.5) - 1.13943427 * jax.random.uniform(seeds[6], (D,), jnp.float32) ** levels(seeds[6], (D,), ((0, 8),), -0.2, 0.2)), 0.8, 2.5),
        "key_gain": jnp.clip(jnp.exp(math.log(2.5) - 1.13943427 * jax.random.uniform(seeds[7], (D,), jnp.float32) ** levels(seeds[7], (D,), ((0, 8),), -0.2, 0.2)), 0.8, 2.5),
    }


def normalize(field, tangent, gain):
    field = field.astype(jnp.float32)
    tangent = tangent.astype(jnp.float32)
    mean_sq = lax.optimization_barrier(jnp.mean(field * field, axis=1, keepdims=True))
    mean_cross = lax.optimization_barrier(jnp.mean(field * tangent, axis=1, keepdims=True))
    inverse = lax.rsqrt(mean_sq + 1e-06)
    normed = (field * inverse * gain).astype(jnp.bfloat16)
    normed_tangent = (gain * (tangent * inverse - field * inverse ** 3 * mean_cross)).astype(jnp.bfloat16)
    return (normed, normed_tangent)

def split_heads(field):
    return field.reshape(field.shape[0], HEADS, HEAD_DIM).transpose(1, 0, 2)

def rounded(field):
    return lax.optimization_barrier(field.astype(jnp.bfloat16)).astype(jnp.float32)

def one_head(items):
    q_head, dq_head, k_head, dk_head, v_head, dv_head = [a.astype(jnp.float32) for a in items]
    scale = HEAD_DIM ** (-0.5)
    scores = jnp.dot(q_head, k_head.T) * scale
    score_tangent = (jnp.dot(dq_head, k_head.T) + jnp.dot(q_head, dk_head.T)) * scale
    top = lax.optimization_barrier(jnp.max(scores, axis=1, keepdims=True))
    weights = jnp.exp(scores - top)
    mixed = weights * score_tangent
    total = lax.optimization_barrier(jnp.sum(weights, axis=1, keepdims=True))
    spread = lax.optimization_barrier(jnp.sum(mixed, axis=1, keepdims=True))
    weights_low = rounded(weights)
    mixed_low = rounded(mixed)
    primal_sum = jnp.dot(weights_low, v_head)
    tangent_sum = jnp.dot(mixed_low, v_head) + jnp.dot(weights_low, dv_head)
    primal = primal_sum / total
    tangent_out = tangent_sum / total - spread / total * primal
    return (primal.astype(jnp.bfloat16), tangent_out.astype(jnp.bfloat16))

def reference(queries, query_tangent, keys, key_tangent, values, value_tangent, query_gain, key_gain):
    normed_q, normed_dq = normalize(queries, query_tangent, query_gain)
    normed_k, normed_dk = normalize(keys, key_tangent, key_gain)
    stacks = tuple((split_heads(a) for a in (normed_q, normed_dq, normed_k, normed_dk, values, value_tangent)))
    primal, tangent_out = lax.map(one_head, stacks)
    attended = primal.transpose(1, 0, 2).reshape(QTOK, D)
    attended_tangent = tangent_out.transpose(1, 0, 2).reshape(QTOK, D)
    return (attended, attended_tangent)
```

```python
import functools

import jax
import jax.numpy as jnp
from jax import lax
from jax.experimental import pallas as pl
from jax.experimental.pallas import tpu as pltpu
from jax.sharding import PartitionSpec as P

HEAD_DIM = 128
MESH = pl.DeviceIdType.MESH
ROWS = 768
BLOCK = 128
QT = 256
EPS = 1e-6
LOG2E = 1.4426950408889634
F32 = jnp.float32
BF16 = jnp.bfloat16


def kernel(
    width,
    n_head,
    n_z,
    q_hbm,
    dq_hbm,
    k_hbm,
    dk_hbm,
    v_hbm,
    dv_hbm,
    qg_ref,
    kg_ref,
    oa_hbm,
    ot_hbm,
    q_in,
    dq_in,
    k_in,
    dk_in,
    stat,
    coef,
    qq,
    q_send,
    kv,
    k_send,
    acc,
    m_ref,
    l_ref,
    sp_ref,
    out,
    in_sem,
    vl_sem,
    st_s,
    st_r,
    yv_s,
    yv_r,
    yk_s,
    yk_r,
    yq_s,
    yq_r,
    z_s,
    z_r,
    o_s,
    o_r,
):
    c = lax.axis_index("ctx")
    h = lax.axis_index("head")
    p = lax.axis_index("dp")
    z = lax.div(c, 2)
    y = lax.rem(c, 2)
    other = 2 * z + 1 - y
    right = (2 * lax.rem(z + 1, n_z) + y, h, p)
    left = (2 * lax.rem(z + n_z - 1, n_z) + y, h, p)
    across = (other, h, p)
    head_peers = [(c, lax.rem(h + i, n_head), p) for i in range(1, n_head)]
    scale = HEAD_DIM ** (-0.5)
    n_q = ROWS // QT
    q_blocks = ROWS // BLOCK

    barrier = pltpu.get_barrier_semaphore()
    for peer in [right, left, across] + head_peers:
        pl.semaphore_signal(barrier, inc=1, device_id=peer, device_id_type=MESH)

    def mine(x):
        return pl.multiple_of((2 * y + x if x < 2 else 4) * HEAD_DIM, HEAD_DIM)

    def theirs(x):
        return pl.multiple_of((2 * (1 - y) + x if x < 2 else 4) * HEAD_DIM, HEAD_DIM)

    loads = [
        pltpu.make_async_copy(src, dst, in_sem.at[i])
        for i, (src, dst) in enumerate(
            ((k_hbm, k_in), (dk_hbm, dk_in), (q_hbm, q_in), (dq_hbm, dq_in))
        )
    ]
    for load in loads:
        load.start()
    v_loads = [
        pltpu.make_async_copy(
            src.at[:, pl.ds(mine(x), HEAD_DIM)],
            kv.at[x, 0, c, :, pl.ds(half * HEAD_DIM, HEAD_DIM)],
            vl_sem.at[x, half],
        )
        for x in range(3)
        for half, src in enumerate((v_hbm, dv_hbm))
    ]
    for load in v_loads:
        load.start()

    def row_sums(a, b):
        field = a.astype(F32)
        tangent = b.astype(F32)
        square = field * field
        cross = field * tangent
        folded = [
            functools.reduce(
                jnp.add, [t[:, i : i + BLOCK] for i in range(0, width, BLOCK)]
            )
            for t in (square, cross)
        ]
        return [jnp.sum(t.T, axis=0, keepdims=True) for t in folded]

    loads[0].wait()
    loads[1].wait()
    sums_k = row_sums(k_in[...], dk_in[...])
    stat[h, 6:7, :] = sums_k[0]
    stat[h, 7:8, :] = jnp.zeros((1, BLOCK), F32)
    stat[h, 14:15, :] = sums_k[1]
    stat[h, 15:16, :] = jnp.zeros((1, BLOCK), F32)
    loads[2].wait()
    loads[3].wait()
    for r in range(q_blocks):
        rows = slice(r * BLOCK, (r + 1) * BLOCK)
        sums_q = row_sums(q_in[rows, :], dq_in[rows, :])
        stat[h, r : r + 1, :] = sums_q[0]
        stat[h, 8 + r : 9 + r, :] = sums_q[1]

    pl.semaphore_wait(barrier, 3 + len(head_peers))

    stat_sends = [
        pltpu.make_async_remote_copy(
            stat.at[h],
            stat.at[h],
            st_s.at[i],
            st_r.at[h],
            device_id=peer,
            device_id_type=MESH,
        )
        for i, peer in enumerate(head_peers)
    ]
    for send in stat_sends:
        send.start()

    yv_sends = [
        pltpu.make_async_remote_copy(
            src.at[:, pl.ds(theirs(x), HEAD_DIM)],
            kv.at[x, 0, c, :, pl.ds(half * HEAD_DIM, HEAD_DIM)],
            yv_s.at[x, half],
            yv_r.at[x, half],
            device_id=across,
            device_id_type=MESH,
        )
        for x in range(3)
        for half, src in enumerate((v_hbm, dv_hbm))
    ]
    for send in yv_sends:
        send.start()

    def ring(x, part, slot, direction, typ, hop):
        return pltpu.make_async_remote_copy(
            kv.at[x, part, slot],
            kv.at[x, part, slot],
            z_s.at[direction, x, part, typ, hop],
            z_r.at[x, part, slot],
            device_id=right if direction == 0 else left,
            device_id_type=MESH,
        )

    def first_hop(x, part, typ):
        slot = c if typ == 0 else other
        for direction in range(2):
            ring(x, part, slot, direction, typ, 0).start()

    for load in v_loads:
        load.wait()
    for x in range(3):
        first_hop(x, 0, 0)

    for i in range(1, n_head):
        sender = lax.rem(h + i, n_head)
        pltpu.make_async_remote_copy(
            stat.at[sender],
            stat.at[sender],
            st_s.at[i - 1],
            st_r.at[sender],
            device_id=head_peers[i - 1],
            device_id_type=MESH,
        ).wait_recv()
    total = functools.reduce(jnp.add, [stat[i] for i in range(n_head)])
    mean = total * (1.0 / (width * n_head))
    inverse = lax.rsqrt(mean[:8] + EPS)
    coef[0:8, :] = inverse
    coef[8:16, :] = inverse * inverse * inverse * mean[8:]

    def normed(field, tangent, gain, inv, third):
        field = field.astype(F32)
        tangent = tangent.astype(F32)
        return (
            (field * inv * gain).astype(BF16),
            (gain * (tangent * inv - field * third)).astype(BF16),
        )

    def spread_rows(row):
        return jnp.broadcast_to(coef[row : row + 1, :], (BLOCK, BLOCK)).T

    inv_k, third_k = spread_rows(6), spread_rows(14)

    def norm_keys(columns, store):
        cols = pl.ds(columns, HEAD_DIM)
        n, dn = normed(k_in[:, cols], dk_in[:, cols], kg_ref[:, cols], inv_k, third_k)
        store[:, 0:HEAD_DIM] = n
        store[:, HEAD_DIM:] = dn

    yk_sends = []
    for x in range(3):
        norm_keys(mine(x), kv.at[x, 1, c])
        if x < 2:
            norm_keys(theirs(x), k_send.at[x])
        send = pltpu.make_async_remote_copy(
            k_send.at[x] if x < 2 else kv.at[x, 1, c],
            kv.at[x, 1, c],
            yk_s.at[x],
            yk_r.at[x],
            device_id=across,
            device_id_type=MESH,
        )
        send.start()
        yk_sends.append(send)
        first_hop(x, 1, 0)

    def arrived_across(x, part):
        if part == 1:
            pltpu.make_async_remote_copy(
                kv.at[x, 1, other],
                kv.at[x, 1, other],
                yk_s.at[x],
                yk_r.at[x],
                device_id=across,
                device_id_type=MESH,
            ).wait_recv()
        else:
            for half, src in enumerate((v_hbm, dv_hbm)):
                pltpu.make_async_remote_copy(
                    src.at[:, pl.ds(theirs(x), HEAD_DIM)],
                    kv.at[x, 0, other, :, pl.ds(half * HEAD_DIM, HEAD_DIM)],
                    yv_s.at[x, half],
                    yv_r.at[x, half],
                    device_id=across,
                    device_id_type=MESH,
                ).wait_recv()

    for x in range(3):
        arrived_across(x, 0)
        first_hop(x, 0, 1)

    def norm_queries(columns, store):
        cols = pl.ds(columns, HEAD_DIM)
        gain = qg_ref[:, cols]
        for r in range(q_blocks):
            rows = slice(r * BLOCK, (r + 1) * BLOCK)
            n, dn = normed(
                q_in[rows, cols], dq_in[rows, cols], gain, spread_rows(r), spread_rows(8 + r)
            )
            store[rows, 0:HEAD_DIM] = dn
            store[rows, HEAD_DIM:] = n

    def q_across(x, i):
        return pltpu.make_async_remote_copy(
            q_send.at[x, pl.ds(i * QT, QT)],
            qq.at[x, pl.ds(ROWS + i * QT, QT)],
            yq_s.at[x, i],
            yq_r.at[x, i],
            device_id=across,
            device_id_type=MESH,
        )

    norm_queries(theirs(0), q_send.at[0])
    for i in range(n_q):
        q_across(0, i).start()
    for x in range(3):
        arrived_across(x, 1)
        first_hop(x, 1, 1)
    norm_queries(theirs(1), q_send.at[1])
    for i in range(n_q):
        q_across(1, i).start()
    for x in range(3):
        norm_queries(mine(x), qq.at[x, pl.ds(0, ROWS)])

    def slot_of(zz, typ):
        return 2 * zz + jnp.where(typ == 0, y, 1 - y)

    last = n_z // 2

    def arrive(x, d, part, typ):
        from_left = slot_of(lax.rem(z + n_z - d, n_z), typ)
        from_right = slot_of(lax.rem(z + d, n_z), typ)

        @pl.when(jnp.logical_or(d < last, typ == 0))
        def _():
            ring(x, part, from_left, 0, typ, 0).wait_recv()

        @pl.when(jnp.logical_or(d < last - 1, jnp.logical_and(d == last - 1, typ == 0)))
        def _():
            ring(x, part, from_left, 0, typ, d).start()

        @pl.when(jnp.logical_or(d < last, typ == 1))
        def _():
            ring(x, part, from_right, 1, typ, 0).wait_recv()

        @pl.when(jnp.logical_or(d < last - 1, jnp.logical_and(d == last - 1, typ == 1)))
        def _():
            ring(x, part, from_right, 1, typ, d).start()

    def own_copy(x, i, which):
        cols = pl.ds(pl.multiple_of(jnp.where(x < 2, 2 * y + x, 4) * HEAD_DIM, HEAD_DIM), HEAD_DIM)
        rows = pl.ds(pl.multiple_of(i * QT, QT), QT)
        return pltpu.make_async_copy(
            out.at[which, x, rows],
            (oa_hbm, ot_hbm)[which].at[rows, cols],
            o_s.at[which, x, i],
        )

    def copy_across(x, i, which):
        cols = pl.ds(pl.multiple_of((2 * y + x) * HEAD_DIM, HEAD_DIM), HEAD_DIM)
        return pltpu.make_async_remote_copy(
            out.at[which, x, pl.ds(pl.multiple_of(ROWS + i * QT, QT), QT)],
            (oa_hbm, ot_hbm)[which].at[pl.ds(pl.multiple_of(i * QT, QT), QT), cols],
            o_s.at[which, x, n_q + i],
            o_r.at[which, x, i],
            device_id=across,
            device_id_type=MESH,
        )

    def tile(x, d, t):
        rows = pl.ds(pl.multiple_of(t * QT, QT), QT)
        far = lax.rem(z + d, n_z)
        near = lax.rem(z + n_z - lax.rem(d, last), n_z)

        @pl.when(jnp.logical_and(d == 1, t >= n_q))
        def _():
            q_across(x, t - n_q).wait_recv()

        @pl.when(d == 1)
        def _():
            acc[rows, :] = jnp.zeros((QT, 2 * HEAD_DIM), F32)
            m_ref[rows, :] = jnp.full((QT, HEAD_DIM), -1e30, F32)
            l_ref[rows, :] = jnp.zeros((QT, HEAD_DIM), F32)
            sp_ref[rows, :] = jnp.zeros((QT, HEAD_DIM), F32)

        pair = qq[x, rows, :]
        query = pair[:, HEAD_DIM:]
        contract = (((1,), (1,)), ((), ()))
        scores, tangents, vals = [], [], []
        for zz in (far, near):
            keys = kv[x, 1, pl.ds(2 * zz, 2)].reshape(2 * BLOCK, 2 * HEAD_DIM)
            vals.append(kv[x, 0, pl.ds(2 * zz, 2)].reshape(2 * BLOCK, 2 * HEAD_DIM))
            scores.append(
                lax.dot_general(
                    query, keys[:, :HEAD_DIM], contract, preferred_element_type=F32
                )
            )
            tangents.append(
                lax.dot_general(pair, keys, contract, preferred_element_type=F32)
            )
        top = jnp.max(jnp.maximum(scores[0], scores[1]), axis=1, keepdims=True)
        before = m_ref[rows, :]
        newest = jnp.maximum(before, top * (scale * LOG2E))
        factor = jnp.exp2(before - newest)
        shift = newest[:, 0:1]
        m_ref[rows, :] = newest
        total_w = l_ref[rows, :] * factor
        total_m = sp_ref[rows, :] * factor
        primal = acc[rows, 0:HEAD_DIM] * factor
        tangent = acc[rows, HEAD_DIM:] * factor
        for s, st, v in zip(scores, tangents, vals):
            w = jnp.exp2(s * (scale * LOG2E) - shift)
            mix = w * st
            for i in range(0, 2 * BLOCK, HEAD_DIM):
                total_w = total_w + w[:, i : i + HEAD_DIM]
                total_m = total_m + mix[:, i : i + HEAD_DIM]
            both = jnp.dot(w.astype(BF16), v, preferred_element_type=F32)
            mixed = jnp.dot(mix.astype(BF16), v[:, :HEAD_DIM], preferred_element_type=F32)
            primal = primal + both[:, :HEAD_DIM]
            tangent = tangent + both[:, HEAD_DIM:] + mixed * scale
        l_ref[rows, :] = total_w
        sp_ref[rows, :] = total_m
        acc[rows, 0:HEAD_DIM] = primal
        acc[rows, HEAD_DIM:] = tangent

        @pl.when(d == last)
        def _():
            whole = jnp.sum(l_ref[rows, :], axis=1, keepdims=True)
            inv = 1.0 / whole
            ratio = jnp.sum(sp_ref[rows, :], axis=1, keepdims=True) * scale * inv
            first = acc[rows, 0:HEAD_DIM] * inv
            out[0, x, rows, :] = first.astype(BF16)
            out[1, x, rows, :] = (acc[rows, HEAD_DIM:] * inv - ratio * first).astype(BF16)

            @pl.when(t < n_q)
            def _():
                for which in range(2):
                    own_copy(x, t, which).start()

            @pl.when(t >= n_q)
            def _():
                for which in range(2):
                    copy_across(x, t - n_q, which).start()

    steps = 3 * last

    def step(g, carry):
        x, d = lax.div(g, last), lax.rem(g, last) + 1
        before = jnp.maximum(g - 1, 0)
        xb, db = lax.div(before, last), lax.rem(before, last) + 1
        tiles = jnp.where(g == 0, 0, jnp.where(xb == 2, n_q, 2 * n_q))

        def sub(i, carry):
            @pl.when(g < steps)
            def _():
                arrive(x, d, lax.div(i, 2), lax.rem(i, 2))

            lax.fori_loop(
                lax.div(tiles * i, 4),
                lax.div(tiles * (i + 1), 4),
                lambda t, carry: (tile(xb, db, t), carry)[1],
                0,
            )
            return carry

        lax.fori_loop(0, 4, sub, 0)
        return carry

    lax.fori_loop(0, steps + 1, step, 0)

    for send in stat_sends + yv_sends + yk_sends:
        send.wait_send()
    for x in range(2):
        for i in range(n_q):
            q_across(x, i).wait_send()

    def drain(i, carry):
        x, part = lax.div(i, 2), lax.rem(i, 2)
        for typ in range(2):
            for hop in range(last):
                for direction in range(2):
                    if hop < last - 1 or direction == typ:
                        ring(x, part, c, direction, typ, hop).wait_send()
        return carry

    lax.fori_loop(0, 6, drain, 0)

    def drain_out(i, carry):
        for which in range(2):
            for x in range(3):
                own_copy(x, i, which).wait()
                if x < 2:
                    copy_across(x, i, which).wait_send()
                    copy_across(x, i, which).wait_recv()
        return carry

    lax.fori_loop(0, n_q, drain_out, 0)


def shards(mesh, queries, query_tangent, keys, key_tangent, values, value_tangent, query_gain, key_gain):
    n_head = mesh.shape["head"]
    n_z = mesh.shape["ctx"] // 2
    width = queries.shape[1]
    dma = pltpu.SemaphoreType.DMA
    anywhere = pl.BlockSpec(memory_space=pl.ANY)
    vmem = pl.BlockSpec(memory_space=pltpu.VMEM)
    n_q = ROWS // QT
    return tuple(pl.pallas_call(
        functools.partial(kernel, width, n_head, n_z),
        out_shape=[jax.ShapeDtypeStruct(queries.shape, BF16)] * 2,
        in_specs=[anywhere] * 6 + [vmem] * 2,
        out_specs=[anywhere] * 2,
        scratch_shapes=[
            pltpu.VMEM((ROWS, width), BF16),
            pltpu.VMEM((ROWS, width), BF16),
            pltpu.VMEM((BLOCK, width), BF16),
            pltpu.VMEM((BLOCK, width), BF16),
            pltpu.VMEM((n_head, 16, BLOCK), F32),
            pltpu.VMEM((16, BLOCK), F32),
            pltpu.VMEM((3, 2 * ROWS, 2 * HEAD_DIM), BF16),
            pltpu.VMEM((2, ROWS, 2 * HEAD_DIM), BF16),
            pltpu.VMEM((3, 2, 2 * n_z, BLOCK, 2 * HEAD_DIM), BF16),
            pltpu.VMEM((2, BLOCK, 2 * HEAD_DIM), BF16),
            pltpu.VMEM((2 * ROWS, 2 * HEAD_DIM), F32),
            pltpu.VMEM((2 * ROWS, HEAD_DIM), F32),
            pltpu.VMEM((2 * ROWS, HEAD_DIM), F32),
            pltpu.VMEM((2 * ROWS, HEAD_DIM), F32),
            pltpu.VMEM((2, 3, 2 * ROWS, HEAD_DIM), BF16),
            dma((4,)),
            dma((3, 2)),
            dma((n_head - 1,)),
            dma((n_head,)),
            dma((3, 2)),
            dma((3, 2)),
            dma((3,)),
            dma((3,)),
            dma((2, n_q)),
            dma((2, n_q)),
            dma((2, 3, 2, 2, n_z // 2)),
            dma((3, 2, 2 * n_z)),
            dma((2, 3, 2 * n_q)),
            dma((2, 2, n_q)),
        ],
        compiler_params=pltpu.CompilerParams(
            collective_id=0, has_side_effects=True, vmem_limit_bytes=62 * 2**20
        ),
        cost_estimate=pl.CostEstimate(
            flops=12 * 5 * ROWS * 16 * BLOCK * HEAD_DIM,
            bytes_accessed=5 * 2**20,
            transcendentals=5 * ROWS * 16 * BLOCK,
        ),
    )(
        queries,
        query_tangent,
        keys,
        key_tangent,
        values,
        value_tangent,
        query_gain.reshape(1, width),
        key_gain.reshape(1, width),
    ))


def solution(mesh):
    rows = P(("dp", "ctx"), "head")
    return jax.shard_map(
        functools.partial(shards, mesh),
        mesh=mesh,
        in_specs=(rows,) * 6 + (P("head"),) * 2,
        out_specs=(rows, rows),
        check_vma=False,
    )
```

```python
import functools

import jax
import jax.numpy as jnp
from jax import lax
from jax.experimental import pallas as pl
from jax.experimental.pallas import tpu as pltpu
from jax.sharding import PartitionSpec as P

HEAD_DIM = 128
MESH = pl.DeviceIdType.MESH
ROWS = 768
BLOCK = 128
QT = 768
EPS = 1e-6
ORDER = ((0, 1), (0, 2), (1, 1), (0, 3), (1, 2), (0, 4), (1, 3), (1, 4), (2, 1), (2, 2), (2, 3), (2, 4))
LOG2E = 1.4426950408889634
F32 = jnp.float32
BF16 = jnp.bfloat16


def by_pair(x, part, d):
    return False if isinstance(x, int) else x > 9


def kernel(
    width,
    n_head,
    n_z,
    q_hbm,
    dq_hbm,
    k_hbm,
    dk_hbm,
    v_hbm,
    dv_hbm,
    qg_ref,
    kg_ref,
    oa_hbm,
    ot_hbm,
    q_in,
    dq_in,
    k_in,
    dk_in,
    stat,
    coef,
    qq,
    q_send,
    kv,
    k_send,
    acc,
    m_ref,
    l_ref,
    sp_ref,
    out,
    in_sem,
    vl_sem,
    st_s,
    st_r,
    yv_s,
    yv_r,
    yk_s,
    yk_r,
    yq_s,
    yq_r,
    z_s,
    z_r,
    p_s,
    o_s,
    o_r,
):
    c = lax.axis_index("ctx")
    h = lax.axis_index("head")
    p = lax.axis_index("dp")
    z = lax.div(c, 2)
    y = lax.rem(c, 2)
    right = (2 * lax.rem(z + 1, n_z) + y, h, p)
    left = (2 * lax.rem(z + n_z - 1, n_z) + y, h, p)
    across = (2 * z + 1 - y, h, p)
    head_peers = [(c, lax.rem(h + i, n_head), p) for i in range(1, n_head)]
    scale = HEAD_DIM ** (-0.5)
    last = n_z // 2
    home = n_z - 1
    n_q = ROWS // QT
    q_blocks = ROWS // BLOCK

    barrier = pltpu.get_barrier_semaphore()
    for peer in [right, left, across] + head_peers:
        pl.semaphore_signal(barrier, inc=1, device_id=peer, device_id_type=MESH)

    def mine(x):
        return pl.multiple_of((2 * y + x if x < 2 else 4) * HEAD_DIM, HEAD_DIM)

    def theirs(x):
        return pl.multiple_of((2 * (1 - y) + x if x < 2 else 4) * HEAD_DIM, HEAD_DIM)

    v_loads = [
        pltpu.make_async_copy(
            src.at[:, pl.ds(mine(x), HEAD_DIM)],
            kv.at[x, 0, home, 0, :, pl.ds(half * HEAD_DIM, HEAD_DIM)],
            vl_sem.at[x, half],
        )
        for x in range(3)
        for half, src in enumerate((v_hbm, dv_hbm))
    ]
    for load in v_loads:
        load.start()

    loads = [
        pltpu.make_async_copy(src, dst, in_sem.at[i])
        for i, (src, dst) in enumerate(
            ((k_hbm, k_in), (dk_hbm, dk_in), (q_hbm, q_in), (dq_hbm, dq_in))
        )
    ]
    for load in loads:
        load.start()
    pl.semaphore_wait(barrier, 3 + len(head_peers))

    yv_sends = [
        pltpu.make_async_remote_copy(
            src.at[:, pl.ds(theirs(x), HEAD_DIM)],
            kv.at[x, 0, home, 1, :, pl.ds(half * HEAD_DIM, HEAD_DIM)],
            yv_s.at[x, half],
            yv_r.at[x, half],
            device_id=across,
            device_id_type=MESH,
        )
        for x in range(3)
        for half, src in enumerate((v_hbm, dv_hbm))
    ]
    for send in yv_sends:
        send.start()

    def ring(x, part, typ, direction, hop):
        src = jnp.where(hop == 0, home, 2 * (hop - 1) + direction)
        dst = jnp.minimum(2 * hop + direction, home - 1)
        return pltpu.make_async_remote_copy(
            kv.at[x, part, src, typ],
            kv.at[x, part, dst, typ],
            z_s.at[direction, x, part, typ, hop],
            z_r.at[x, part, dst, typ],
            device_id=right if direction == 0 else left,
            device_id_type=MESH,
        )

    def first_hop(x, part, typ):
        for direction in range(2):
            ring(x, part, typ, direction, 0).start()

    for x in range(3):
        v_loads[2 * x].wait()
        v_loads[2 * x + 1].wait()
        first_hop(x, 0, 0)

    def row_sums(a, b):
        field = a.astype(F32)
        tangent = b.astype(F32)
        square = field * field
        cross = field * tangent
        folded = [
            functools.reduce(
                jnp.add, [t[:, i : i + BLOCK] for i in range(0, width, BLOCK)]
            )
            for t in (square, cross)
        ]
        return [jnp.sum(t.T, axis=0, keepdims=True) for t in folded]

    loads[0].wait()
    loads[1].wait()
    sums_k = row_sums(k_in[...], dk_in[...])
    stat[h, 6:7, :] = sums_k[0]
    stat[h, 7:8, :] = jnp.zeros((1, BLOCK), F32)
    stat[h, 14:15, :] = sums_k[1]
    stat[h, 15:16, :] = jnp.zeros((1, BLOCK), F32)
    loads[2].wait()
    loads[3].wait()
    for r in range(q_blocks):
        rows = slice(r * BLOCK, (r + 1) * BLOCK)
        sums_q = row_sums(q_in[rows, :], dq_in[rows, :])
        stat[h, r : r + 1, :] = sums_q[0]
        stat[h, 8 + r : 9 + r, :] = sums_q[1]

    stat_sends = [
        pltpu.make_async_remote_copy(
            stat.at[h],
            stat.at[h],
            st_s.at[i],
            st_r.at[h],
            device_id=peer,
            device_id_type=MESH,
        )
        for i, peer in enumerate(head_peers)
    ]
    for send in stat_sends:
        send.start()

    def arrived_across(x, part):
        if part == 1:
            pltpu.make_async_remote_copy(
                kv.at[x, 1, home, 0],
                kv.at[x, 1, home, 1],
                yk_s.at[x],
                yk_r.at[x],
                device_id=across,
                device_id_type=MESH,
            ).wait_recv()
        else:
            for half, src in enumerate((v_hbm, dv_hbm)):
                pltpu.make_async_remote_copy(
                    src.at[:, pl.ds(theirs(x), HEAD_DIM)],
                    kv.at[x, 0, home, 1, :, pl.ds(half * HEAD_DIM, HEAD_DIM)],
                    yv_s.at[x, half],
                    yv_r.at[x, half],
                    device_id=across,
                    device_id_type=MESH,
                ).wait_recv()

    for x in range(3):
        arrived_across(x, 0)
        if not by_pair(x, 0, 1):
            first_hop(x, 0, 1)

    for i in range(1, n_head):
        sender = lax.rem(h + i, n_head)
        pltpu.make_async_remote_copy(
            stat.at[sender],
            stat.at[sender],
            st_s.at[i - 1],
            st_r.at[sender],
            device_id=head_peers[i - 1],
            device_id_type=MESH,
        ).wait_recv()
    total = functools.reduce(jnp.add, [stat[i] for i in range(n_head)])
    mean = total * (1.0 / (width * n_head))
    inverse = lax.rsqrt(mean[:8] + EPS)
    coef[0:8, :] = inverse
    coef[8:16, :] = inverse * inverse * inverse * mean[8:]

    def normed(field, tangent, gain, inv, third):
        field = field.astype(F32)
        tangent = tangent.astype(F32)
        return (
            (field * inv * gain).astype(BF16),
            (gain * (tangent * inv - field * third)).astype(BF16),
        )

    def spread_rows(row):
        return jnp.broadcast_to(coef[row : row + 1, :], (BLOCK, BLOCK)).T

    inv_k, third_k = spread_rows(6), spread_rows(14)

    def norm_keys(columns, store):
        cols = pl.ds(columns, HEAD_DIM)
        n, dn = normed(k_in[:, cols], dk_in[:, cols], kg_ref[cols].reshape(1, HEAD_DIM), inv_k, third_k)
        store[:, 0:HEAD_DIM] = n
        store[:, HEAD_DIM:] = dn

    yk_sends = []
    for x in range(3):
        norm_keys(mine(x), kv.at[x, 1, home, 0])
        if x < 2:
            norm_keys(theirs(x), k_send.at[x])
        send = pltpu.make_async_remote_copy(
            k_send.at[x] if x < 2 else kv.at[x, 1, home, 0],
            kv.at[x, 1, home, 1],
            yk_s.at[x],
            yk_r.at[x],
            device_id=across,
            device_id_type=MESH,
        )
        send.start()
        yk_sends.append(send)
        first_hop(x, 1, 0)

    def norm_queries(columns, store):
        cols = pl.ds(columns, HEAD_DIM)
        gain = qg_ref[cols].reshape(1, HEAD_DIM)
        for r in range(q_blocks):
            rows = slice(r * BLOCK, (r + 1) * BLOCK)
            n, dn = normed(
                q_in[rows, cols], dq_in[rows, cols], gain, spread_rows(r), spread_rows(8 + r)
            )
            store[rows, 0:HEAD_DIM] = dn
            store[rows, HEAD_DIM:] = n

    def q_across(x, i):
        return pltpu.make_async_remote_copy(
            q_send.at[x, pl.ds(i * QT, QT)],
            qq.at[x, pl.ds(ROWS + i * QT, QT)],
            yq_s.at[x, i],
            yq_r.at[x, i],
            device_id=across,
            device_id_type=MESH,
        )

    norm_queries(theirs(0), q_send.at[0])
    for i in range(n_q):
        q_across(0, i).start()
    for x in range(3):
        arrived_across(x, 1)
        if not by_pair(x, 1, 1):
            first_hop(x, 1, 1)
    norm_queries(theirs(1), q_send.at[1])
    for i in range(n_q):
        q_across(1, i).start()
    for x in range(3):
        norm_queries(mine(x), qq.at[x, pl.ds(0, ROWS)])

    def over(x, part, d, direction):
        pos = jnp.minimum(2 * (d - 1) + direction, home - 1)
        return pltpu.make_async_remote_copy(
            kv.at[x, part, pos, 0],
            kv.at[x, part, pos, 1],
            p_s.at[x, part, pos],
            z_r.at[x, part, pos, 1],
            device_id=across,
            device_id_type=MESH,
        )

    def arrive(x, d, part, typ):
        paired = by_pair(x, part, d)
        paired_next = by_pair(x, part, d + 1)
        for direction in range(2):
            here = jnp.logical_or(d < last, typ == direction)
            on = jnp.logical_or(d < last - 1, jnp.logical_and(d == last - 1, typ == direction))

            from_pair = jnp.logical_and(paired, typ == 1)
            by_ring = jnp.logical_and(here, jnp.logical_not(from_pair))
            by_other = jnp.logical_and(
                from_pair, jnp.logical_or(d < last, direction == 0)
            )

            @pl.when(by_ring)
            def _():
                ring(x, part, typ, direction, d - 1).wait_recv()

            @pl.when(by_other)
            def _():
                over(x, part, d, direction).wait_recv()

            @pl.when(jnp.logical_and(on, jnp.logical_not(jnp.logical_and(paired_next, typ == 1))))
            def _():
                ring(x, part, typ, direction, d).start()

            @pl.when(jnp.logical_and(jnp.logical_and(paired, typ == 0), here))
            def _():
                over(x, part, d, direction).start()

    def own_copy(x, i, which):
        cols = pl.ds(pl.multiple_of(jnp.where(x < 2, 2 * y + x, 4) * HEAD_DIM, HEAD_DIM), HEAD_DIM)
        rows = pl.ds(pl.multiple_of(i * QT, QT), QT)
        return pltpu.make_async_copy(
            out.at[which, x, rows],
            (oa_hbm, ot_hbm)[which].at[rows, cols],
            o_s.at[which, x, i],
        )

    def copy_across(x, i, which):
        cols = pl.ds(pl.multiple_of((2 * y + x) * HEAD_DIM, HEAD_DIM), HEAD_DIM)
        return pltpu.make_async_remote_copy(
            out.at[which, x, pl.ds(pl.multiple_of(ROWS + i * QT, QT), QT)],
            (oa_hbm, ot_hbm)[which].at[pl.ds(pl.multiple_of(i * QT, QT), QT), cols],
            o_s.at[which, x, n_q + i],
            o_r.at[which, x, i],
            device_id=across,
            device_id_type=MESH,
        )

    def tile(x, d, t):
        rows = pl.ds(pl.multiple_of(t * QT, QT), QT)
        @pl.when(jnp.logical_and(d == 1, t >= n_q))
        def _():
            q_across(x, t - n_q).wait_recv()

        @pl.when(d == 1)
        def _():
            acc[x, rows, :] = jnp.zeros((QT, 2 * HEAD_DIM), F32)
            m_ref[x, rows, :] = jnp.full((QT, HEAD_DIM), -1e30, F32)
            l_ref[x, rows, :] = jnp.zeros((QT, HEAD_DIM), F32)
            sp_ref[x, rows, :] = jnp.zeros((QT, HEAD_DIM), F32)

        pair = qq[x, rows, :]
        query = pair[:, HEAD_DIM:]
        contract = (((1,), (1,)), ((), ()))
        keys = kv[x, 1, pl.ds(2 * (d - 1), 2)].reshape(4 * BLOCK, 2 * HEAD_DIM)
        vals = kv[x, 0, pl.ds(2 * (d - 1), 2)].reshape(4 * BLOCK, 2 * HEAD_DIM)
        scores = lax.dot_general(query, keys[:, :HEAD_DIM], contract, preferred_element_type=F32)
        slopes = lax.dot_general(pair, keys, contract, preferred_element_type=F32)
        top = jnp.max(scores, axis=1, keepdims=True)
        before = m_ref[x, rows, :]
        newest = jnp.maximum(before, top * (scale * LOG2E))
        factor = jnp.exp2(before - newest)
        m_ref[x, rows, :] = newest
        total_w = l_ref[x, rows, :] * factor
        total_m = sp_ref[x, rows, :] * factor
        w = jnp.exp2(scores * (scale * LOG2E) - newest[:, 0:1])
        mix = w * slopes
        for i in range(0, 4 * BLOCK, HEAD_DIM):
            total_w = total_w + w[:, i : i + HEAD_DIM]
            total_m = total_m + mix[:, i : i + HEAD_DIM]
        both = jnp.dot(w.astype(BF16), vals, preferred_element_type=F32)
        mixed = jnp.dot(mix.astype(BF16), vals[:, :HEAD_DIM], preferred_element_type=F32)
        primal = acc[x, rows, 0:HEAD_DIM] * factor + both[:, :HEAD_DIM]
        tangent = acc[x, rows, HEAD_DIM:] * factor + both[:, HEAD_DIM:] + mixed * scale
        l_ref[x, rows, :] = total_w
        sp_ref[x, rows, :] = total_m
        acc[x, rows, 0:HEAD_DIM] = primal
        acc[x, rows, HEAD_DIM:] = tangent

        @pl.when(d == last)
        def _():
            whole = jnp.sum(l_ref[x, rows, :], axis=1, keepdims=True)
            inv = 1.0 / whole
            ratio = jnp.sum(sp_ref[x, rows, :], axis=1, keepdims=True) * scale * inv
            first = acc[x, rows, 0:HEAD_DIM] * inv
            out[0, x, rows, :] = first.astype(BF16)
            out[1, x, rows, :] = (acc[x, rows, HEAD_DIM:] * inv - ratio * first).astype(BF16)

            @pl.when(t < n_q)
            def _():
                for which in range(2):
                    own_copy(x, t, which).start()

            @pl.when(t >= n_q)
            def _():
                for which in range(2):
                    copy_across(x, t - n_q, which).start()

    steps = 3 * last

    def turn(g):
        order = ORDER
        x, d = order[-1]
        for i, (xi, di) in enumerate(order[:-1]):
            x = jnp.where(g == i, xi, x)
            d = jnp.where(g == i, di, d)
        return x, d

    def step(g, carry):
        x, d = turn(g)
        xb, db = turn(jnp.maximum(g - 1, 0))
        tiles = jnp.where(g == 0, 0, jnp.where(xb == 2, n_q, 2 * n_q))

        def sub(i, carry):
            @pl.when(g < steps)
            def _():
                arrive(x, d, lax.div(i, 2), lax.rem(i, 2))

            lax.fori_loop(
                lax.div(tiles * i, 4),
                lax.div(tiles * (i + 1), 4),
                lambda t, carry: (
                    tile(xb, db, jnp.where(db == last, tiles - 1 - t, t)),
                    carry,
                )[1],
                0,
            )
            return carry

        lax.fori_loop(0, 4, sub, 0)
        return carry

    lax.fori_loop(0, steps + 1, step, 0)

    for send in stat_sends + yv_sends + yk_sends:
        send.wait_send()
    for x in range(2):
        for i in range(n_q):
            q_across(x, i).wait_send()

    def drain(i, carry):
        x, part = lax.div(i, 2), lax.rem(i, 2)
        for typ in range(2):
            for hop in range(last):
                for direction in range(2):
                    if hop < last - 1 or direction == typ:

                        @pl.when(jnp.logical_not(jnp.logical_and(by_pair(x, part, hop + 1), typ == 1)))
                        def _():
                            ring(x, part, typ, direction, hop).wait_send()

                    if typ == 0 and (hop < last - 1 or direction == 0):

                        @pl.when(by_pair(x, part, hop + 1))
                        def _():
                            over(x, part, hop + 1, direction).wait_send()

        return carry

    lax.fori_loop(0, 6, drain, 0)

    def drain_out(i, carry):
        for which in range(2):
            for x in range(3):
                own_copy(x, i, which).wait()
                if x < 2:
                    copy_across(x, i, which).wait_send()
                    copy_across(x, i, which).wait_recv()
        return carry

    lax.fori_loop(0, n_q, drain_out, 0)


def copies(oa_src, ot_src, oa_dst, ot_dst, held, load_sem, store_sem):
    parts = 2
    size = ROWS // parts
    loads, stores = [], []
    for i in range(parts):
        rows = pl.ds(i * size, size)
        for j, (src, dst) in enumerate(((oa_src, oa_dst), (ot_src, ot_dst))):
            loads.append(pltpu.make_async_copy(src.at[rows], held.at[j, rows], load_sem.at[j, i]))
            stores.append(pltpu.make_async_copy(held.at[j, rows], dst.at[rows], store_sem.at[j, i]))
    for load in loads:
        load.start()
    for load, store in zip(loads, stores):
        load.wait()
        store.start()
    for store in stores:
        store.wait()


def settle(first, second):
    anywhere = pl.BlockSpec(memory_space=pl.ANY)
    return tuple(
        pl.pallas_call(
            copies,
            out_shape=[jax.ShapeDtypeStruct(first.shape, BF16)] * 2,
            in_specs=[anywhere] * 2,
            out_specs=[anywhere] * 2,
            scratch_shapes=[
                pltpu.VMEM((2,) + first.shape, BF16),
                pltpu.SemaphoreType.DMA((2, 2)),
                pltpu.SemaphoreType.DMA((2, 2)),
            ],
            compiler_params=pltpu.CompilerParams(vmem_limit_bytes=62 * 2**20),
        )(first, second)
    )


def shards(mesh, queries, query_tangent, keys, key_tangent, values, value_tangent, query_gain, key_gain):
    n_head = mesh.shape["head"]
    n_z = mesh.shape["ctx"] // 2
    width = queries.shape[1]
    dma = pltpu.SemaphoreType.DMA
    anywhere = pl.BlockSpec(memory_space=pl.ANY)
    vmem = pl.BlockSpec(memory_space=pltpu.VMEM)
    n_q = ROWS // QT
    results = pl.pallas_call(
        functools.partial(kernel, width, n_head, n_z),
        out_shape=[jax.ShapeDtypeStruct(queries.shape, BF16)] * 2,
        in_specs=[anywhere] * 6 + [vmem] * 2,
        out_specs=[anywhere] * 2,
        scratch_shapes=[
            pltpu.VMEM((ROWS, width), BF16),
            pltpu.VMEM((ROWS, width), BF16),
            pltpu.VMEM((BLOCK, width), BF16),
            pltpu.VMEM((BLOCK, width), BF16),
            pltpu.VMEM((n_head, 16, BLOCK), F32),
            pltpu.VMEM((16, BLOCK), F32),
            pltpu.VMEM((3, 2 * ROWS, 2 * HEAD_DIM), BF16),
            pltpu.VMEM((2, ROWS, 2 * HEAD_DIM), BF16),
            pltpu.VMEM((3, 2, n_z, 2, BLOCK, 2 * HEAD_DIM), BF16),
            pltpu.VMEM((2, BLOCK, 2 * HEAD_DIM), BF16),
            pltpu.VMEM((3, 2 * ROWS, 2 * HEAD_DIM), F32),
            pltpu.VMEM((3, 2 * ROWS, HEAD_DIM), F32),
            pltpu.VMEM((3, 2 * ROWS, HEAD_DIM), F32),
            pltpu.VMEM((3, 2 * ROWS, HEAD_DIM), F32),
            pltpu.VMEM((2, 3, 2 * ROWS, HEAD_DIM), BF16),
            dma((4,)),
            dma((3, 2)),
            dma((n_head - 1,)),
            dma((n_head,)),
            dma((3, 2)),
            dma((3, 2)),
            dma((3,)),
            dma((3,)),
            dma((2, n_q)),
            dma((2, n_q)),
            dma((2, 3, 2, 2, n_z // 2)),
            dma((3, 2, n_z, 2)),
            dma((3, 2, n_z)),
            dma((2, 3, 2 * n_q)),
            dma((2, 2, n_q)),
        ],
        compiler_params=pltpu.CompilerParams(
            collective_id=0, has_side_effects=True, vmem_limit_bytes=62 * 2**20
        ),
        cost_estimate=pl.CostEstimate(
            flops=12 * 5 * ROWS * 16 * BLOCK * HEAD_DIM,
            bytes_accessed=5 * 2**20,
            transcendentals=5 * ROWS * 16 * BLOCK,
        ),
    )(
        queries,
        query_tangent,
        keys,
        key_tangent,
        values,
        value_tangent,
        query_gain,
        key_gain,
    )
    return settle(*results)


def solution(mesh):
    rows = P(("dp", "ctx"), "head")
    return jax.shard_map(
        functools.partial(shards, mesh),
        mesh=mesh,
        in_specs=(rows,) * 6 + (P("head"),) * 2,
        out_specs=(rows, rows),
        check_vma=False,
    )
```

```python
import functools

import jax
import jax.numpy as jnp
from jax import lax
from jax.experimental import pallas as pl
from jax.experimental.pallas import tpu as pltpu
from jax.sharding import PartitionSpec as P

HEAD_DIM = 128
MESH = pl.DeviceIdType.MESH
ROWS = 768
BLOCK = 128
QT = 768
EPS = 1e-6
ORDER = ((0, 1), (0, 2), (1, 1), (0, 3), (1, 2), (0, 4), (1, 3), (2, 1), (1, 4), (2, 2), (2, 3), (2, 4))
SECOND_STARTS, THIRD_STARTS = 0, 5
LOG2E = 1.4426950408889634
F32 = jnp.float32
BF16 = jnp.bfloat16


def kernel(
    width,
    n_head,
    n_z,
    q_hbm,
    dq_hbm,
    k_hbm,
    dk_hbm,
    v_hbm,
    dv_hbm,
    qg_ref,
    kg_ref,
    oa_hbm,
    ot_hbm,
    q_in,
    dq_in,
    k_in,
    dk_in,
    stat,
    coef,
    qq,
    q_send,
    kv,
    k_send,
    acc,
    m_ref,
    l_ref,
    sp_ref,
    out,
    in_sem,
    vl_sem,
    st_s,
    st_r,
    yv_s,
    yv_r,
    yk_s,
    yk_r,
    yq_s,
    yq_r,
    z_s,
    z_r,
    o_s,
    o_r,
):
    c = lax.axis_index("ctx")
    h = lax.axis_index("head")
    p = lax.axis_index("dp")
    z = lax.div(c, 2)
    y = lax.rem(c, 2)
    right = (2 * lax.rem(z + 1, n_z) + y, h, p)
    left = (2 * lax.rem(z + n_z - 1, n_z) + y, h, p)
    across = (2 * z + 1 - y, h, p)
    head_peers = [(c, lax.rem(h + i, n_head), p) for i in range(1, n_head)]
    scale = HEAD_DIM ** (-0.5)
    last = n_z // 2
    home = n_z - 1
    n_q = ROWS // QT
    q_blocks = ROWS // BLOCK

    barrier = pltpu.get_barrier_semaphore()
    for peer in [right, left, across] + head_peers:
        pl.semaphore_signal(barrier, inc=1, device_id=peer, device_id_type=MESH)

    def mine(x):
        return pl.multiple_of((2 * y + x if x < 2 else 4) * HEAD_DIM, HEAD_DIM)

    def theirs(x):
        return pl.multiple_of((2 * (1 - y) + x if x < 2 else 4) * HEAD_DIM, HEAD_DIM)

    v_loads = [
        pltpu.make_async_copy(
            src.at[:, pl.ds(mine(x), HEAD_DIM)],
            kv.at[x, 0, home, 0, :, pl.ds(half * HEAD_DIM, HEAD_DIM)],
            vl_sem.at[x, half],
        )
        for x in range(3)
        for half, src in enumerate((v_hbm, dv_hbm))
    ]
    for load in v_loads:
        load.start()

    loads = [
        pltpu.make_async_copy(src, dst, in_sem.at[i])
        for i, (src, dst) in enumerate(
            ((k_hbm, k_in), (dk_hbm, dk_in), (q_hbm, q_in), (dq_hbm, dq_in))
        )
    ]
    for load in loads:
        load.start()
    pl.semaphore_wait(barrier, 3 + len(head_peers))

    yv_sends = [
        pltpu.make_async_remote_copy(
            src.at[:, pl.ds(theirs(x), HEAD_DIM)],
            kv.at[x, 0, home, 1, :, pl.ds(half * HEAD_DIM, HEAD_DIM)],
            yv_s.at[x, half],
            yv_r.at[x, half],
            device_id=across,
            device_id_type=MESH,
        )
        for x in range(3)
        for half, src in enumerate((v_hbm, dv_hbm))
    ]
    for send in yv_sends[:4]:
        send.start()

    def ring(x, part, typ, direction, hop):
        src = jnp.where(hop == 0, home, 2 * (hop - 1) + direction)
        dst = jnp.minimum(2 * hop + direction, home - 1)
        return pltpu.make_async_remote_copy(
            kv.at[x, part, src, typ],
            kv.at[x, part, dst, typ],
            z_s.at[direction, x, part, typ, hop],
            z_r.at[x, part, dst, typ],
            device_id=right if direction == 0 else left,
            device_id_type=MESH,
        )

    def first_hop(x, part, typ):
        for direction in range(2):
            ring(x, part, typ, direction, 0).start()

    for x in range(3):
        v_loads[2 * x].wait()
        v_loads[2 * x + 1].wait()
        first_hop(x, 0, 0)

    def row_sums(a, b):
        field = a.astype(F32)
        tangent = b.astype(F32)
        square = field * field
        cross = field * tangent
        folded = [
            functools.reduce(
                jnp.add, [t[:, i : i + BLOCK] for i in range(0, width, BLOCK)]
            )
            for t in (square, cross)
        ]
        return [jnp.sum(t.T, axis=0, keepdims=True) for t in folded]

    loads[0].wait()
    loads[1].wait()
    sums_k = row_sums(k_in[...], dk_in[...])
    stat[h, 6:7, :] = sums_k[0]
    stat[h, 7:8, :] = jnp.zeros((1, BLOCK), F32)
    stat[h, 14:15, :] = sums_k[1]
    stat[h, 15:16, :] = jnp.zeros((1, BLOCK), F32)
    loads[2].wait()
    loads[3].wait()
    for r in range(q_blocks):
        rows = slice(r * BLOCK, (r + 1) * BLOCK)
        sums_q = row_sums(q_in[rows, :], dq_in[rows, :])
        stat[h, r : r + 1, :] = sums_q[0]
        stat[h, 8 + r : 9 + r, :] = sums_q[1]

    stat_sends = [
        pltpu.make_async_remote_copy(
            stat.at[h],
            stat.at[h],
            st_s.at[i],
            st_r.at[h],
            device_id=peer,
            device_id_type=MESH,
        )
        for i, peer in enumerate(head_peers)
    ]
    for send in stat_sends:
        send.start()

    def arrived_across(x, part):
        if part == 1:
            pltpu.make_async_remote_copy(
                kv.at[x, 1, home, 0],
                kv.at[x, 1, home, 1],
                yk_s.at[x],
                yk_r.at[x],
                device_id=across,
                device_id_type=MESH,
            ).wait_recv()
        else:
            for half, src in enumerate((v_hbm, dv_hbm)):
                pltpu.make_async_remote_copy(
                    src.at[:, pl.ds(theirs(x), HEAD_DIM)],
                    kv.at[x, 0, home, 1, :, pl.ds(half * HEAD_DIM, HEAD_DIM)],
                    yv_s.at[x, half],
                    yv_r.at[x, half],
                    device_id=across,
                    device_id_type=MESH,
                ).wait_recv()

    arrived_across(0, 0)
    first_hop(0, 0, 1)

    for i in range(1, n_head):
        sender = lax.rem(h + i, n_head)
        pltpu.make_async_remote_copy(
            stat.at[sender],
            stat.at[sender],
            st_s.at[i - 1],
            st_r.at[sender],
            device_id=head_peers[i - 1],
            device_id_type=MESH,
        ).wait_recv()
    total = functools.reduce(jnp.add, [stat[i] for i in range(n_head)])
    mean = total * (1.0 / (width * n_head))
    inverse = lax.rsqrt(mean[:8] + EPS)
    coef[0:8, :] = inverse
    coef[8:16, :] = inverse * inverse * inverse * mean[8:]

    def normed(field, tangent, gain, inv, third):
        field = field.astype(F32)
        tangent = tangent.astype(F32)
        return (
            (field * inv * gain).astype(BF16),
            (gain * (tangent * inv - field * third)).astype(BF16),
        )

    def spread_rows(row):
        return jnp.broadcast_to(coef[row : row + 1, :], (BLOCK, BLOCK)).T

    inv_k, third_k = spread_rows(6), spread_rows(14)

    def norm_keys(columns, store):
        cols = pl.ds(columns, HEAD_DIM)
        n, dn = normed(k_in[:, cols], dk_in[:, cols], kg_ref[cols].reshape(1, HEAD_DIM), inv_k, third_k)
        store[:, 0:HEAD_DIM] = n
        store[:, HEAD_DIM:] = dn

    yk_sends = [
        pltpu.make_async_remote_copy(
            k_send.at[x] if x < 2 else kv.at[x, 1, home, 0],
            kv.at[x, 1, home, 1],
            yk_s.at[x],
            yk_r.at[x],
            device_id=across,
            device_id_type=MESH,
        )
        for x in range(3)
    ]
    for x in range(2):
        norm_keys(theirs(x), k_send.at[x])
        yk_sends[x].start()
        norm_keys(mine(x), kv.at[x, 1, home, 0])
        if x == 0:
            first_hop(0, 1, 0)
    norm_keys(mine(2), kv.at[2, 1, home, 0])

    def norm_queries(columns, store):
        cols = pl.ds(columns, HEAD_DIM)
        gain = qg_ref[cols].reshape(1, HEAD_DIM)
        for r in range(q_blocks):
            rows = slice(r * BLOCK, (r + 1) * BLOCK)
            n, dn = normed(
                q_in[rows, cols], dq_in[rows, cols], gain, spread_rows(r), spread_rows(8 + r)
            )
            store[rows, 0:HEAD_DIM] = dn
            store[rows, HEAD_DIM:] = n

    def q_across(x, i):
        return pltpu.make_async_remote_copy(
            q_send.at[x, pl.ds(i * QT, QT)],
            qq.at[x, pl.ds(ROWS + i * QT, QT)],
            yq_s.at[x, i],
            yq_r.at[x, i],
            device_id=across,
            device_id_type=MESH,
        )

    norm_queries(theirs(0), q_send.at[0])
    for i in range(n_q):
        q_across(0, i).start()
    arrived_across(0, 1)
    first_hop(0, 1, 1)
    norm_queries(theirs(1), q_send.at[1])
    for x in range(3):
        norm_queries(mine(x), qq.at[x, pl.ds(0, ROWS)])

    def arrive(x, d, part, typ):
        for direction in range(2):

            @pl.when(jnp.logical_or(d < last, typ == direction))
            def _():
                ring(x, part, typ, direction, d - 1).wait_recv()

            @pl.when(jnp.logical_or(d < last - 1, jnp.logical_and(d == last - 1, typ == direction)))
            def _():
                ring(x, part, typ, direction, d).start()

    def own_copy(x, i, which):
        cols = pl.ds(pl.multiple_of(jnp.where(x < 2, 2 * y + x, 4) * HEAD_DIM, HEAD_DIM), HEAD_DIM)
        rows = pl.ds(pl.multiple_of(i * QT, QT), QT)
        return pltpu.make_async_copy(
            out.at[which, x, rows],
            (oa_hbm, ot_hbm)[which].at[rows, cols],
            o_s.at[which, x, i],
        )

    def copy_across(x, i, which):
        cols = pl.ds(pl.multiple_of((2 * y + x) * HEAD_DIM, HEAD_DIM), HEAD_DIM)
        return pltpu.make_async_remote_copy(
            out.at[which, x, pl.ds(pl.multiple_of(ROWS + i * QT, QT), QT)],
            (oa_hbm, ot_hbm)[which].at[pl.ds(pl.multiple_of(i * QT, QT), QT), cols],
            o_s.at[which, x, n_q + i],
            o_r.at[which, x, i],
            device_id=across,
            device_id_type=MESH,
        )

    def tile(x, d, t):
        rows = pl.ds(pl.multiple_of(t * QT, QT), QT)
        @pl.when(jnp.logical_and(d == 1, t >= n_q))
        def _():
            q_across(x, t - n_q).wait_recv()

        @pl.when(d == 1)
        def _():
            acc[x, rows, :] = jnp.zeros((QT, 2 * HEAD_DIM), F32)
            m_ref[x, rows, :] = jnp.full((QT, HEAD_DIM), -1e30, F32)
            l_ref[x, rows, :] = jnp.zeros((QT, HEAD_DIM), F32)
            sp_ref[x, rows, :] = jnp.zeros((QT, HEAD_DIM), F32)

        pair = qq[x, rows, :]
        query = pair[:, HEAD_DIM:]
        contract = (((1,), (1,)), ((), ()))
        keys = kv[x, 1, pl.ds(2 * (d - 1), 2)].reshape(4 * BLOCK, 2 * HEAD_DIM)
        vals = kv[x, 0, pl.ds(2 * (d - 1), 2)].reshape(4 * BLOCK, 2 * HEAD_DIM)
        scores = lax.dot_general(query, keys[:, :HEAD_DIM], contract, preferred_element_type=F32)
        slopes = lax.dot_general(pair, keys, contract, preferred_element_type=F32)
        top = jnp.max(scores, axis=1, keepdims=True)
        before = m_ref[x, rows, :]
        newest = jnp.maximum(before, top * (scale * LOG2E))
        factor = jnp.exp2(before - newest)
        m_ref[x, rows, :] = newest
        total_w = l_ref[x, rows, :] * factor
        total_m = sp_ref[x, rows, :] * factor
        w = jnp.exp2(scores * (scale * LOG2E) - newest[:, 0:1])
        mix = w * slopes
        for i in range(0, 4 * BLOCK, HEAD_DIM):
            total_w = total_w + w[:, i : i + HEAD_DIM]
            total_m = total_m + mix[:, i : i + HEAD_DIM]
        both = jnp.dot(w.astype(BF16), vals, preferred_element_type=F32)
        mixed = jnp.dot(mix.astype(BF16), vals[:, :HEAD_DIM], preferred_element_type=F32)
        primal = acc[x, rows, 0:HEAD_DIM] * factor + both[:, :HEAD_DIM]
        tangent = acc[x, rows, HEAD_DIM:] * factor + both[:, HEAD_DIM:] + mixed * scale
        l_ref[x, rows, :] = total_w
        sp_ref[x, rows, :] = total_m
        acc[x, rows, 0:HEAD_DIM] = primal
        acc[x, rows, HEAD_DIM:] = tangent

        @pl.when(d == last)
        def _():
            whole = jnp.sum(l_ref[x, rows, :], axis=1, keepdims=True)
            inv = 1.0 / whole
            ratio = jnp.sum(sp_ref[x, rows, :], axis=1, keepdims=True) * scale * inv
            first = acc[x, rows, 0:HEAD_DIM] * inv
            out[0, x, rows, :] = first.astype(BF16)
            out[1, x, rows, :] = (acc[x, rows, HEAD_DIM:] * inv - ratio * first).astype(BF16)

            @pl.when(t < n_q)
            def _():
                for which in range(2):
                    own_copy(x, t, which).start()

            @pl.when(t >= n_q)
            def _():
                for which in range(2):
                    copy_across(x, t - n_q, which).start()

    steps = 3 * last

    def turn(g):
        order = ORDER
        x, d = order[-1]
        for i, (xi, di) in enumerate(order[:-1]):
            x = jnp.where(g == i, xi, x)
            d = jnp.where(g == i, di, d)
        return x, d

    def step(g, carry):
        x, d = turn(g)
        xb, db = turn(jnp.maximum(g - 1, 0))
        tiles = jnp.where(g == 0, 0, jnp.where(xb == 2, n_q, 2 * n_q))

        @pl.when(g == 1)
        def _():
            for send in yv_sends[4:] + yk_sends[2:]:
                send.start()

        @pl.when(g == 2)
        def _():
            for i in range(n_q):
                q_across(1, i).start()

        def sub(i, carry):
            lax.fori_loop(
                lax.div(tiles * i + 3, 4),
                lax.div(tiles * (i + 1) + 3, 4),
                lambda t, carry: (
                    tile(xb, db, jnp.where(db == last, tiles - 1 - t, t)),
                    carry,
                )[1],
                0,
            )

            @pl.when(g < steps)
            def _():
                arrive(x, d, lax.div(i, 2), lax.rem(i, 2))

            for head, start in ((1, SECOND_STARTS), (2, THIRD_STARTS)):
                for k, (part, typ) in enumerate(((0, 1), (1, 0), (1, 1))):

                    @pl.when(jnp.logical_and(g == start, i == k))
                    def _(head=head, part=part, typ=typ):
                        if typ == 1:
                            arrived_across(head, part)
                        first_hop(head, part, typ)

            return carry

        lax.fori_loop(0, 4, sub, 0)
        return carry

    lax.fori_loop(0, steps + 1, step, 0)

    for send in stat_sends + yv_sends + yk_sends:
        send.wait_send()
    for x in range(2):
        for i in range(n_q):
            q_across(x, i).wait_send()

    def drain(i, carry):
        x, part = lax.div(i, 2), lax.rem(i, 2)
        for typ in range(2):
            for hop in range(last):
                for direction in range(2):
                    if hop < last - 1 or direction == typ:
                        ring(x, part, typ, direction, hop).wait_send()
        return carry

    lax.fori_loop(0, 6, drain, 0)

    def drain_out(i, carry):
        for which in range(2):
            for x in range(3):
                own_copy(x, i, which).wait()
                if x < 2:
                    copy_across(x, i, which).wait_send()
                    copy_across(x, i, which).wait_recv()
        return carry

    lax.fori_loop(0, n_q, drain_out, 0)


def copies(oa_src, ot_src, oa_dst, ot_dst, held, load_sem, store_sem):
    parts = 2
    size = ROWS // parts
    loads, stores = [], []
    for i in range(parts):
        rows = pl.ds(i * size, size)
        for j, (src, dst) in enumerate(((oa_src, oa_dst), (ot_src, ot_dst))):
            loads.append(pltpu.make_async_copy(src.at[rows], held.at[j, rows], load_sem.at[j, i]))
            stores.append(pltpu.make_async_copy(held.at[j, rows], dst.at[rows], store_sem.at[j, i]))
    for load in loads:
        load.start()
    for load, store in zip(loads, stores):
        load.wait()
        store.start()
    for store in stores:
        store.wait()


def settle(first, second):
    anywhere = pl.BlockSpec(memory_space=pl.ANY)
    return tuple(
        pl.pallas_call(
            copies,
            out_shape=[jax.ShapeDtypeStruct(first.shape, BF16)] * 2,
            in_specs=[anywhere] * 2,
            out_specs=[anywhere] * 2,
            scratch_shapes=[
                pltpu.VMEM((2,) + first.shape, BF16),
                pltpu.SemaphoreType.DMA((2, 2)),
                pltpu.SemaphoreType.DMA((2, 2)),
            ],
            compiler_params=pltpu.CompilerParams(vmem_limit_bytes=62 * 2**20),
        )(first, second)
    )


def shards(mesh, queries, query_tangent, keys, key_tangent, values, value_tangent, query_gain, key_gain):
    n_head = mesh.shape["head"]
    n_z = mesh.shape["ctx"] // 2
    width = queries.shape[1]
    dma = pltpu.SemaphoreType.DMA
    anywhere = pl.BlockSpec(memory_space=pl.ANY)
    vmem = pl.BlockSpec(memory_space=pltpu.VMEM)
    n_q = ROWS // QT
    results = pl.pallas_call(
        functools.partial(kernel, width, n_head, n_z),
        out_shape=[jax.ShapeDtypeStruct(queries.shape, BF16)] * 2,
        in_specs=[anywhere] * 6 + [vmem] * 2,
        out_specs=[anywhere] * 2,
        scratch_shapes=[
            pltpu.VMEM((ROWS, width), BF16),
            pltpu.VMEM((ROWS, width), BF16),
            pltpu.VMEM((BLOCK, width), BF16),
            pltpu.VMEM((BLOCK, width), BF16),
            pltpu.VMEM((n_head, 16, BLOCK), F32),
            pltpu.VMEM((16, BLOCK), F32),
            pltpu.VMEM((3, 2 * ROWS, 2 * HEAD_DIM), BF16),
            pltpu.VMEM((2, ROWS, 2 * HEAD_DIM), BF16),
            pltpu.VMEM((3, 2, n_z, 2, BLOCK, 2 * HEAD_DIM), BF16),
            pltpu.VMEM((2, BLOCK, 2 * HEAD_DIM), BF16),
            pltpu.VMEM((3, 2 * ROWS, 2 * HEAD_DIM), F32),
            pltpu.VMEM((3, 2 * ROWS, HEAD_DIM), F32),
            pltpu.VMEM((3, 2 * ROWS, HEAD_DIM), F32),
            pltpu.VMEM((3, 2 * ROWS, HEAD_DIM), F32),
            pltpu.VMEM((2, 3, 2 * ROWS, HEAD_DIM), BF16),
            dma((4,)),
            dma((3, 2)),
            dma((n_head - 1,)),
            dma((n_head,)),
            dma((3, 2)),
            dma((3, 2)),
            dma((3,)),
            dma((3,)),
            dma((2, n_q)),
            dma((2, n_q)),
            dma((2, 3, 2, 2, n_z // 2)),
            dma((3, 2, n_z, 2)),
            dma((2, 3, 2 * n_q)),
            dma((2, 2, n_q)),
        ],
        compiler_params=pltpu.CompilerParams(
            collective_id=0, has_side_effects=True, vmem_limit_bytes=62 * 2**20
        ),
        cost_estimate=pl.CostEstimate(
            flops=12 * 5 * ROWS * 16 * BLOCK * HEAD_DIM,
            bytes_accessed=5 * 2**20,
            transcendentals=5 * ROWS * 16 * BLOCK,
        ),
    )(
        queries,
        query_tangent,
        keys,
        key_tangent,
        values,
        value_tangent,
        query_gain,
        key_gain,
    )
    return settle(*results)


def solution(mesh):
    rows = P(("dp", "ctx"), "head")
    return jax.shard_map(
        functools.partial(shards, mesh),
        mesh=mesh,
        in_specs=(rows,) * 6 + (P("head"),) * 2,
        out_specs=(rows, rows),
        check_vma=False,
    )
```

```python
import functools

import jax
import jax.numpy as jnp
from jax import lax
from jax.experimental import pallas as pl
from jax.experimental.pallas import tpu as pltpu
from jax.sharding import PartitionSpec as P

HEAD_DIM = 128
MESH = pl.DeviceIdType.MESH
ROWS = 768
BLOCK = 128
QT = 768
EPS = 1e-6
ORDER = ((0, 1), (0, 2), (1, 1), (0, 3), (1, 2), (0, 4), (1, 3), (2, 1), (1, 4), (2, 2), (2, 3), (2, 4))
SECOND_STARTS, THIRD_STARTS = 0, 5
LOG2E = 1.4426950408889634
F32 = jnp.float32
BF16 = jnp.bfloat16


def kernel(
    width,
    n_head,
    n_z,
    q_hbm,
    dq_hbm,
    k_hbm,
    dk_hbm,
    v_hbm,
    dv_hbm,
    qg_ref,
    kg_ref,
    oa_hbm,
    ot_hbm,
    q_in,
    dq_in,
    k_in,
    dk_in,
    stat,
    coef,
    qq,
    q_send,
    kv,
    k_send,
    acc,
    m_ref,
    l_ref,
    sp_ref,
    out,
    in_sem,
    vl_sem,
    st_s,
    st_r,
    yv_s,
    yv_r,
    yk_s,
    yk_r,
    yq_s,
    yq_r,
    z_s,
    z_r,
    o_s,
    o_r,
):
    c = lax.axis_index("ctx")
    h = lax.axis_index("head")
    p = lax.axis_index("dp")
    z = lax.div(c, 2)
    y = lax.rem(c, 2)
    right = (2 * lax.rem(z + 1, n_z) + y, h, p)
    left = (2 * lax.rem(z + n_z - 1, n_z) + y, h, p)
    across = (2 * z + 1 - y, h, p)
    head_peers = [(c, lax.rem(h + i, n_head), p) for i in range(1, n_head)]
    scale = HEAD_DIM ** (-0.5)
    last = n_z // 2
    home = n_z - 1
    n_q = ROWS // QT
    q_blocks = ROWS // BLOCK

    def mine(x):
        return pl.multiple_of((2 * y + x if x < 2 else 4) * HEAD_DIM, HEAD_DIM)

    def theirs(x):
        return pl.multiple_of((2 * (1 - y) + x if x < 2 else 4) * HEAD_DIM, HEAD_DIM)

    v_loads = [
        pltpu.make_async_copy(
            src.at[:, pl.ds(mine(x), HEAD_DIM)],
            kv.at[x, 0, home, 0, :, pl.ds(half * HEAD_DIM, HEAD_DIM)],
            vl_sem.at[x, half],
        )
        for x in range(3)
        for half, src in enumerate((v_hbm, dv_hbm))
    ]
    for load in v_loads:
        load.start()

    loads = [
        pltpu.make_async_copy(src, dst, in_sem.at[i])
        for i, (src, dst) in enumerate(
            ((k_hbm, k_in), (dk_hbm, dk_in), (q_hbm, q_in), (dq_hbm, dq_in))
        )
    ]
    for load in loads:
        load.start()
    barrier = pltpu.get_barrier_semaphore()
    for peer in [right, left, across] + head_peers:
        pl.semaphore_signal(barrier, inc=1, device_id=peer, device_id_type=MESH)

    pl.semaphore_wait(barrier, 3 + len(head_peers))

    yv_sends = [
        pltpu.make_async_remote_copy(
            src.at[:, pl.ds(theirs(x), HEAD_DIM)],
            kv.at[x, 0, home, 1, :, pl.ds(half * HEAD_DIM, HEAD_DIM)],
            yv_s.at[x, half],
            yv_r.at[x, half],
            device_id=across,
            device_id_type=MESH,
        )
        for x in range(3)
        for half, src in enumerate((v_hbm, dv_hbm))
    ]
    for send in yv_sends[:4]:
        send.start()

    def ring(x, part, typ, direction, hop):
        src = jnp.where(hop == 0, home, 2 * (hop - 1) + direction)
        dst = jnp.minimum(2 * hop + direction, home - 1)
        return pltpu.make_async_remote_copy(
            kv.at[x, part, src, typ],
            kv.at[x, part, dst, typ],
            z_s.at[direction, x, part, typ, hop],
            z_r.at[x, part, dst, typ],
            device_id=right if direction == 0 else left,
            device_id_type=MESH,
        )

    def first_hop(x, part, typ):
        for direction in range(2):
            ring(x, part, typ, direction, 0).start()

    for x in range(3):
        v_loads[2 * x].wait()
        v_loads[2 * x + 1].wait()
        first_hop(x, 0, 0)

    def row_sums(a, b):
        field = a.astype(F32)
        tangent = b.astype(F32)
        square = field * field
        cross = field * tangent
        folded = [
            functools.reduce(
                jnp.add, [t[:, i : i + BLOCK] for i in range(0, width, BLOCK)]
            )
            for t in (square, cross)
        ]
        return [jnp.sum(t.T, axis=0, keepdims=True) for t in folded]

    loads[0].wait()
    loads[1].wait()
    sums_k = row_sums(k_in[...], dk_in[...])
    stat[h, 6:7, :] = sums_k[0]
    stat[h, 7:8, :] = jnp.zeros((1, BLOCK), F32)
    stat[h, 14:15, :] = sums_k[1]
    stat[h, 15:16, :] = jnp.zeros((1, BLOCK), F32)
    loads[2].wait()
    loads[3].wait()
    for r in range(q_blocks):
        rows = slice(r * BLOCK, (r + 1) * BLOCK)
        sums_q = row_sums(q_in[rows, :], dq_in[rows, :])
        stat[h, r : r + 1, :] = sums_q[0]
        stat[h, 8 + r : 9 + r, :] = sums_q[1]

    stat_sends = [
        pltpu.make_async_remote_copy(
            stat.at[h],
            stat.at[h],
            st_s.at[i],
            st_r.at[h],
            device_id=peer,
            device_id_type=MESH,
        )
        for i, peer in enumerate(head_peers)
    ]
    for send in stat_sends:
        send.start()

    def arrived_across(x, part):
        if part == 1:
            pltpu.make_async_remote_copy(
                kv.at[x, 1, home, 0],
                kv.at[x, 1, home, 1],
                yk_s.at[x],
                yk_r.at[x],
                device_id=across,
                device_id_type=MESH,
            ).wait_recv()
        else:
            for half, src in enumerate((v_hbm, dv_hbm)):
                pltpu.make_async_remote_copy(
                    src.at[:, pl.ds(theirs(x), HEAD_DIM)],
                    kv.at[x, 0, home, 1, :, pl.ds(half * HEAD_DIM, HEAD_DIM)],
                    yv_s.at[x, half],
                    yv_r.at[x, half],
                    device_id=across,
                    device_id_type=MESH,
                ).wait_recv()

    arrived_across(0, 0)
    first_hop(0, 0, 1)

    for i in range(1, n_head):
        sender = lax.rem(h + i, n_head)
        pltpu.make_async_remote_copy(
            stat.at[sender],
            stat.at[sender],
            st_s.at[i - 1],
            st_r.at[sender],
            device_id=head_peers[i - 1],
            device_id_type=MESH,
        ).wait_recv()
    total = functools.reduce(jnp.add, [stat[i] for i in range(n_head)])
    mean = total * (1.0 / (width * n_head))
    inverse = lax.rsqrt(mean[:8] + EPS)
    coef[0:8, :] = inverse
    coef[8:16, :] = inverse * inverse * inverse * mean[8:]

    def normed(field, tangent, gain, inv, third):
        field = field.astype(F32)
        tangent = tangent.astype(F32)
        return (
            (field * inv * gain).astype(BF16),
            (gain * (tangent * inv - field * third)).astype(BF16),
        )

    def spread_rows(row):
        return jnp.broadcast_to(coef[row : row + 1, :], (BLOCK, BLOCK)).T

    inv_k, third_k = spread_rows(6), spread_rows(14)

    def norm_keys(columns, store):
        cols = pl.ds(columns, HEAD_DIM)
        n, dn = normed(k_in[:, cols], dk_in[:, cols], kg_ref[cols].reshape(1, HEAD_DIM), inv_k, third_k)
        store[:, 0:HEAD_DIM] = n
        store[:, HEAD_DIM:] = dn

    yk_sends = [
        pltpu.make_async_remote_copy(
            k_send.at[x] if x < 2 else kv.at[x, 1, home, 0],
            kv.at[x, 1, home, 1],
            yk_s.at[x],
            yk_r.at[x],
            device_id=across,
            device_id_type=MESH,
        )
        for x in range(3)
    ]
    for x in range(2):
        norm_keys(theirs(x), k_send.at[x])
        yk_sends[x].start()
        norm_keys(mine(x), kv.at[x, 1, home, 0])
        if x == 0:
            first_hop(0, 1, 0)
    norm_keys(mine(2), kv.at[2, 1, home, 0])

    def norm_queries(columns, store):
        cols = pl.ds(columns, HEAD_DIM)
        gain = qg_ref[cols].reshape(1, HEAD_DIM)
        for r in range(q_blocks):
            rows = slice(r * BLOCK, (r + 1) * BLOCK)
            n, dn = normed(
                q_in[rows, cols], dq_in[rows, cols], gain, spread_rows(r), spread_rows(8 + r)
            )
            store[rows, 0:HEAD_DIM] = dn
            store[rows, HEAD_DIM:] = n

    def q_across(x, i):
        return pltpu.make_async_remote_copy(
            q_send.at[x, pl.ds(i * QT, QT)],
            qq.at[x, pl.ds(ROWS + i * QT, QT)],
            yq_s.at[x, i],
            yq_r.at[x, i],
            device_id=across,
            device_id_type=MESH,
        )

    norm_queries(theirs(0), q_send.at[0])
    for i in range(n_q):
        q_across(0, i).start()
    arrived_across(0, 1)
    first_hop(0, 1, 1)
    norm_queries(theirs(1), q_send.at[1])
    for x in range(3):
        norm_queries(mine(x), qq.at[x, pl.ds(0, ROWS)])

    def arrive(x, d, part, typ):
        for direction in range(2):

            @pl.when(jnp.logical_or(d < last, typ == direction))
            def _():
                ring(x, part, typ, direction, d - 1).wait_recv()

            @pl.when(jnp.logical_or(d < last - 1, jnp.logical_and(d == last - 1, typ == direction)))
            def _():
                ring(x, part, typ, direction, d).start()

    def own_copy(x, i, which):
        cols = pl.ds(pl.multiple_of(jnp.where(x < 2, 2 * y + x, 4) * HEAD_DIM, HEAD_DIM), HEAD_DIM)
        rows = pl.ds(pl.multiple_of(i * QT, QT), QT)
        return pltpu.make_async_copy(
            out.at[which, x, rows],
            (oa_hbm, ot_hbm)[which].at[rows, cols],
            o_s.at[which, x, i],
        )

    def copy_across(x, i, which):
        cols = pl.ds(pl.multiple_of((2 * y + x) * HEAD_DIM, HEAD_DIM), HEAD_DIM)
        return pltpu.make_async_remote_copy(
            out.at[which, x, pl.ds(pl.multiple_of(ROWS + i * QT, QT), QT)],
            (oa_hbm, ot_hbm)[which].at[pl.ds(pl.multiple_of(i * QT, QT), QT), cols],
            o_s.at[which, x, n_q + i],
            o_r.at[which, x, i],
            device_id=across,
            device_id_type=MESH,
        )

    def tile(x, d, t):
        rows = pl.ds(pl.multiple_of(t * QT, QT), QT)
        @pl.when(jnp.logical_and(d == 1, t >= n_q))
        def _():
            q_across(x, t - n_q).wait_recv()

        @pl.when(d == 1)
        def _():
            acc[x, rows, :] = jnp.zeros((QT, 2 * HEAD_DIM), F32)
            m_ref[x, rows, :] = jnp.full((QT, HEAD_DIM), -1e30, F32)
            l_ref[x, rows, :] = jnp.zeros((QT, HEAD_DIM), F32)
            sp_ref[x, rows, :] = jnp.zeros((QT, HEAD_DIM), F32)

        pair = qq[x, rows, :]
        query = pair[:, HEAD_DIM:]
        contract = (((1,), (1,)), ((), ()))
        keys = kv[x, 1, pl.ds(2 * (d - 1), 2)].reshape(4 * BLOCK, 2 * HEAD_DIM)
        vals = kv[x, 0, pl.ds(2 * (d - 1), 2)].reshape(4 * BLOCK, 2 * HEAD_DIM)
        scores = lax.dot_general(query, keys[:, :HEAD_DIM], contract, preferred_element_type=F32)
        slopes = lax.dot_general(pair, keys, contract, preferred_element_type=F32)
        top = jnp.max(scores, axis=1, keepdims=True)
        before = m_ref[x, rows, :]
        newest = jnp.maximum(before, top * (scale * LOG2E))
        factor = jnp.exp2(before - newest)
        m_ref[x, rows, :] = newest
        total_w = l_ref[x, rows, :] * factor
        total_m = sp_ref[x, rows, :] * factor
        w = jnp.exp2(scores * (scale * LOG2E) - newest[:, 0:1])
        mix = w * slopes
        for i in range(0, 4 * BLOCK, HEAD_DIM):
            total_w = total_w + w[:, i : i + HEAD_DIM]
            total_m = total_m + mix[:, i : i + HEAD_DIM]
        both = jnp.dot(w.astype(BF16), vals, preferred_element_type=F32)
        mixed = jnp.dot(mix.astype(BF16), vals[:, :HEAD_DIM], preferred_element_type=F32)
        primal = acc[x, rows, 0:HEAD_DIM] * factor + both[:, :HEAD_DIM]
        tangent = acc[x, rows, HEAD_DIM:] * factor + both[:, HEAD_DIM:] + mixed * scale
        l_ref[x, rows, :] = total_w
        sp_ref[x, rows, :] = total_m
        acc[x, rows, 0:HEAD_DIM] = primal
        acc[x, rows, HEAD_DIM:] = tangent

        @pl.when(d == last)
        def _():
            whole = jnp.sum(l_ref[x, rows, :], axis=1, keepdims=True)
            inv = 1.0 / whole
            ratio = jnp.sum(sp_ref[x, rows, :], axis=1, keepdims=True) * scale * inv
            first = acc[x, rows, 0:HEAD_DIM] * inv
            out[0, x, rows, :] = first.astype(BF16)
            out[1, x, rows, :] = (acc[x, rows, HEAD_DIM:] * inv - ratio * first).astype(BF16)

            @pl.when(t < n_q)
            def _():
                for which in range(2):
                    own_copy(x, t, which).start()

            @pl.when(t >= n_q)
            def _():
                for which in range(2):
                    copy_across(x, t - n_q, which).start()

    steps = 3 * last

    def turn(g):
        order = ORDER
        x, d = order[-1]
        for i, (xi, di) in enumerate(order[:-1]):
            x = jnp.where(g == i, xi, x)
            d = jnp.where(g == i, di, d)
        return x, d

    def step(g, carry):
        x, d = turn(g)
        xb, db = turn(jnp.maximum(g - 1, 0))
        tiles = jnp.where(g == 0, 0, jnp.where(xb == 2, n_q, 2 * n_q))

        @pl.when(g == 1)
        def _():
            for send in yv_sends[4:] + yk_sends[2:]:
                send.start()

        @pl.when(g == 2)
        def _():
            for i in range(n_q):
                q_across(1, i).start()

        def sub(i, carry):
            lax.fori_loop(
                lax.div(tiles * i + 3, 4),
                lax.div(tiles * (i + 1) + 3, 4),
                lambda t, carry: (
                    tile(xb, db, jnp.where(db == last, tiles - 1 - t, t)),
                    carry,
                )[1],
                0,
            )

            @pl.when(g < steps)
            def _():
                arrive(x, d, lax.div(i, 2), lax.rem(i, 2))

            for head, start in ((1, SECOND_STARTS), (2, THIRD_STARTS)):
                for k, (part, typ) in enumerate(((0, 1), (1, 0), (1, 1))):

                    @pl.when(jnp.logical_and(g == start, i == k))
                    def _(head=head, part=part, typ=typ):
                        if typ == 1:
                            arrived_across(head, part)
                        first_hop(head, part, typ)

            return carry

        lax.fori_loop(0, 4, sub, 0)
        return carry

    lax.fori_loop(0, steps + 1, step, 0)

    for send in stat_sends + yv_sends + yk_sends:
        send.wait_send()
    for x in range(2):
        for i in range(n_q):
            q_across(x, i).wait_send()

    def drain(i, carry):
        x, part = lax.div(i, 2), lax.rem(i, 2)
        for typ in range(2):
            for hop in range(last):
                for direction in range(2):
                    if hop < last - 1 or direction == typ:
                        ring(x, part, typ, direction, hop).wait_send()
        return carry

    lax.fori_loop(0, 6, drain, 0)

    def drain_out(i, carry):
        for which in range(2):
            for x in range(3):
                own_copy(x, i, which).wait()
                if x < 2:
                    copy_across(x, i, which).wait_send()
                    copy_across(x, i, which).wait_recv()
        return carry

    lax.fori_loop(0, n_q, drain_out, 0)


def copies(oa_src, ot_src, oa_dst, ot_dst, sem):
    moves = [
        pltpu.make_async_copy(src, dst, sem.at[j])
        for j, (src, dst) in enumerate(((oa_src, oa_dst), (ot_src, ot_dst)))
    ]
    for move in moves:
        move.start()
    for move in moves:
        move.wait()


def settle(first, second):
    anywhere = pl.BlockSpec(memory_space=pl.ANY)
    return tuple(
        pl.pallas_call(
            copies,
            out_shape=[jax.ShapeDtypeStruct(first.shape, BF16)] * 2,
            in_specs=[anywhere] * 2,
            out_specs=[anywhere] * 2,
            scratch_shapes=[pltpu.SemaphoreType.DMA((2,))],
            compiler_params=pltpu.CompilerParams(vmem_limit_bytes=4 * 2**20),
        )(first, second)
    )


def shards(mesh, queries, query_tangent, keys, key_tangent, values, value_tangent, query_gain, key_gain):
    n_head = mesh.shape["head"]
    n_z = mesh.shape["ctx"] // 2
    width = queries.shape[1]
    dma = pltpu.SemaphoreType.DMA
    anywhere = pl.BlockSpec(memory_space=pl.ANY)
    vmem = pl.BlockSpec(memory_space=pltpu.VMEM)
    n_q = ROWS // QT
    results = pl.pallas_call(
        functools.partial(kernel, width, n_head, n_z),
        out_shape=[pltpu.VMEM(queries.shape, BF16)] * 2,
        in_specs=[anywhere] * 6 + [vmem] * 2,
        out_specs=[anywhere] * 2,
        scratch_shapes=[
            pltpu.VMEM((ROWS, width), BF16),
            pltpu.VMEM((ROWS, width), BF16),
            pltpu.VMEM((BLOCK, width), BF16),
            pltpu.VMEM((BLOCK, width), BF16),
            pltpu.VMEM((n_head, 16, BLOCK), F32),
            pltpu.VMEM((16, BLOCK), F32),
            pltpu.VMEM((3, 2 * ROWS, 2 * HEAD_DIM), BF16),
            pltpu.VMEM((2, ROWS, 2 * HEAD_DIM), BF16),
            pltpu.VMEM((3, 2, n_z, 2, BLOCK, 2 * HEAD_DIM), BF16),
            pltpu.VMEM((2, BLOCK, 2 * HEAD_DIM), BF16),
            pltpu.VMEM((3, 2 * ROWS, 2 * HEAD_DIM), F32),
            pltpu.VMEM((3, 2 * ROWS, HEAD_DIM), F32),
            pltpu.VMEM((3, 2 * ROWS, HEAD_DIM), F32),
            pltpu.VMEM((3, 2 * ROWS, HEAD_DIM), F32),
            pltpu.VMEM((2, 3, 2 * ROWS, HEAD_DIM), BF16),
            dma((4,)),
            dma((3, 2)),
            dma((n_head - 1,)),
            dma((n_head,)),
            dma((3, 2)),
            dma((3, 2)),
            dma((3,)),
            dma((3,)),
            dma((2, n_q)),
            dma((2, n_q)),
            dma((2, 3, 2, 2, n_z // 2)),
            dma((3, 2, n_z, 2)),
            dma((2, 3, 2 * n_q)),
            dma((2, 2, n_q)),
        ],
        compiler_params=pltpu.CompilerParams(
            collective_id=0, has_side_effects=True, vmem_limit_bytes=58 * 2**20
        ),
        cost_estimate=pl.CostEstimate(
            flops=12 * 5 * ROWS * 16 * BLOCK * HEAD_DIM,
            bytes_accessed=5 * 2**20,
            transcendentals=5 * ROWS * 16 * BLOCK,
        ),
    )(
        queries,
        query_tangent,
        keys,
        key_tangent,
        values,
        value_tangent,
        query_gain,
        key_gain,
    )
    return settle(*results)


def solution(mesh):
    rows = P(("dp", "ctx"), "head")
    return jax.shard_map(
        functools.partial(shards, mesh),
        mesh=mesh,
        in_specs=(rows,) * 6 + (P("head"),) * 2,
        out_specs=(rows, rows),
        check_vma=False,
    )
```

```python
import functools

import jax
import jax.numpy as jnp
from jax import lax
from jax.experimental import pallas as pl
from jax.experimental.pallas import tpu as pltpu
from jax.sharding import PartitionSpec as P

HEAD_DIM = 128
MESH = pl.DeviceIdType.MESH
ROWS = 768
BLOCK = 128
QT = 768
EPS = 1e-6
ORDER = ((0, 1), (0, 2), (1, 1), (0, 3), (1, 2), (0, 4), (1, 3), (2, 1), (1, 4), (2, 2), (2, 3), (2, 4))
SECOND_STARTS, THIRD_STARTS = 0, 5
LOG2E = 1.4426950408889634
F32 = jnp.float32
BF16 = jnp.bfloat16


def kernel(
    width,
    n_head,
    n_z,
    q_hbm,
    dq_hbm,
    k_hbm,
    dk_hbm,
    v_hbm,
    dv_hbm,
    qg_ref,
    kg_ref,
    oa_hbm,
    ot_hbm,
    q_in,
    dq_in,
    k_in,
    dk_in,
    stat,
    coef,
    qq,
    q_send,
    kv,
    k_send,
    acc,
    m_ref,
    l_ref,
    sp_ref,
    out,
    in_sem,
    vl_sem,
    st_s,
    st_r,
    yv_s,
    yv_r,
    yk_s,
    yk_r,
    yq_s,
    yq_r,
    z_s,
    z_r,
    o_s,
    o_r,
):
    c = lax.axis_index("ctx")
    h = lax.axis_index("head")
    p = lax.axis_index("dp")
    z = lax.div(c, 2)
    y = lax.rem(c, 2)
    right = (2 * lax.rem(z + 1, n_z) + y, h, p)
    left = (2 * lax.rem(z + n_z - 1, n_z) + y, h, p)
    across = (2 * z + 1 - y, h, p)
    head_peers = [(c, lax.rem(h + i, n_head), p) for i in range(1, n_head)]
    scale = HEAD_DIM ** (-0.5)
    last = n_z // 2
    home = 0
    n_q = ROWS // QT
    q_blocks = ROWS // BLOCK

    def mine(x):
        return pl.multiple_of((2 * y + x if x < 2 else 4) * HEAD_DIM, HEAD_DIM)

    def theirs(x):
        return pl.multiple_of((2 * (1 - y) + x if x < 2 else 4) * HEAD_DIM, HEAD_DIM)

    v_loads = [
        pltpu.make_async_copy(
            src.at[:, pl.ds(mine(x), HEAD_DIM)],
            kv.at[x, 0, home, 0, :, pl.ds(half * HEAD_DIM, HEAD_DIM)],
            vl_sem.at[x, half],
        )
        for x in range(3)
        for half, src in enumerate((v_hbm, dv_hbm))
    ]
    for load in v_loads:
        load.start()

    loads = [
        pltpu.make_async_copy(src, dst, in_sem.at[i])
        for i, (src, dst) in enumerate(
            ((k_hbm, k_in), (dk_hbm, dk_in), (q_hbm, q_in), (dq_hbm, dq_in))
        )
    ]
    for load in loads:
        load.start()
    barrier = pltpu.get_barrier_semaphore()
    for peer in [right, left, across] + head_peers:
        pl.semaphore_signal(barrier, inc=1, device_id=peer, device_id_type=MESH)

    pl.semaphore_wait(barrier, 3 + len(head_peers))

    yv_sends = [
        pltpu.make_async_remote_copy(
            src.at[:, pl.ds(theirs(x), HEAD_DIM)],
            kv.at[x, 0, home, 1, :, pl.ds(half * HEAD_DIM, HEAD_DIM)],
            yv_s.at[x, half],
            yv_r.at[x, half],
            device_id=across,
            device_id_type=MESH,
        )
        for x in range(3)
        for half, src in enumerate((v_hbm, dv_hbm))
    ]
    for send in yv_sends[:4]:
        send.start()

    def ring(x, part, typ, direction, hop):
        src = jnp.where(hop == 0, home, 2 * hop - 1 + direction)
        dst = jnp.minimum(2 * hop + 1 + direction, n_z - 1)
        return pltpu.make_async_remote_copy(
            kv.at[x, part, src, typ],
            kv.at[x, part, dst, typ],
            z_s.at[direction, x, part, typ, hop],
            z_r.at[x, part, dst, typ],
            device_id=right if direction == 0 else left,
            device_id_type=MESH,
        )

    def first_hop(x, part, typ):
        for direction in range(2):
            ring(x, part, typ, direction, 0).start()

    for x in range(3):
        v_loads[2 * x].wait()
        v_loads[2 * x + 1].wait()
        first_hop(x, 0, 0)

    def row_sums(a, b):
        field = a.astype(F32)
        tangent = b.astype(F32)
        square = field * field
        cross = field * tangent
        folded = [
            functools.reduce(
                jnp.add, [t[:, i : i + BLOCK] for i in range(0, width, BLOCK)]
            )
            for t in (square, cross)
        ]
        return [jnp.sum(t.T, axis=0, keepdims=True) for t in folded]

    loads[0].wait()
    loads[1].wait()
    sums_k = row_sums(k_in[...], dk_in[...])
    stat[h, 6:7, :] = sums_k[0]
    stat[h, 7:8, :] = jnp.zeros((1, BLOCK), F32)
    stat[h, 14:15, :] = sums_k[1]
    stat[h, 15:16, :] = jnp.zeros((1, BLOCK), F32)
    loads[2].wait()
    loads[3].wait()
    for r in range(q_blocks):
        rows = slice(r * BLOCK, (r + 1) * BLOCK)
        sums_q = row_sums(q_in[rows, :], dq_in[rows, :])
        stat[h, r : r + 1, :] = sums_q[0]
        stat[h, 8 + r : 9 + r, :] = sums_q[1]

    stat_sends = [
        pltpu.make_async_remote_copy(
            stat.at[h],
            stat.at[h],
            st_s.at[i],
            st_r.at[h],
            device_id=peer,
            device_id_type=MESH,
        )
        for i, peer in enumerate(head_peers)
    ]
    for send in stat_sends:
        send.start()

    def arrived_across(x, part):
        if part == 1:
            pltpu.make_async_remote_copy(
                kv.at[x, 1, home, 0],
                kv.at[x, 1, home, 1],
                yk_s.at[x],
                yk_r.at[x],
                device_id=across,
                device_id_type=MESH,
            ).wait_recv()
        else:
            for half, src in enumerate((v_hbm, dv_hbm)):
                pltpu.make_async_remote_copy(
                    src.at[:, pl.ds(theirs(x), HEAD_DIM)],
                    kv.at[x, 0, home, 1, :, pl.ds(half * HEAD_DIM, HEAD_DIM)],
                    yv_s.at[x, half],
                    yv_r.at[x, half],
                    device_id=across,
                    device_id_type=MESH,
                ).wait_recv()

    arrived_across(0, 0)
    first_hop(0, 0, 1)

    for i in range(1, n_head):
        sender = lax.rem(h + i, n_head)
        pltpu.make_async_remote_copy(
            stat.at[sender],
            stat.at[sender],
            st_s.at[i - 1],
            st_r.at[sender],
            device_id=head_peers[i - 1],
            device_id_type=MESH,
        ).wait_recv()
    total = functools.reduce(jnp.add, [stat[i] for i in range(n_head)])
    mean = total * (1.0 / (width * n_head))
    inverse = lax.rsqrt(mean[:8] + EPS)
    coef[0:8, :] = inverse
    coef[8:16, :] = inverse * inverse * inverse * mean[8:]

    def normed(field, tangent, gain, inv, third):
        field = field.astype(F32)
        tangent = tangent.astype(F32)
        return (
            (field * inv * gain).astype(BF16),
            (gain * (tangent * inv - field * third)).astype(BF16),
        )

    def spread_rows(row):
        return jnp.broadcast_to(coef[row : row + 1, :], (BLOCK, BLOCK)).T

    inv_k, third_k = spread_rows(6), spread_rows(14)

    def norm_keys(columns, store):
        cols = pl.ds(columns, HEAD_DIM)
        n, dn = normed(k_in[:, cols], dk_in[:, cols], kg_ref[cols].reshape(1, HEAD_DIM), inv_k, third_k)
        store[:, 0:HEAD_DIM] = n
        store[:, HEAD_DIM:] = dn

    yk_sends = [
        pltpu.make_async_remote_copy(
            k_send.at[x] if x < 2 else kv.at[x, 1, home, 0],
            kv.at[x, 1, home, 1],
            yk_s.at[x],
            yk_r.at[x],
            device_id=across,
            device_id_type=MESH,
        )
        for x in range(3)
    ]
    for x in range(2):
        norm_keys(theirs(x), k_send.at[x])
        yk_sends[x].start()
        norm_keys(mine(x), kv.at[x, 1, home, 0])
        if x == 0:
            first_hop(0, 1, 0)
    norm_keys(mine(2), kv.at[2, 1, home, 0])

    def norm_queries(columns, store):
        cols = pl.ds(columns, HEAD_DIM)
        gain = qg_ref[cols].reshape(1, HEAD_DIM)
        for r in range(q_blocks):
            rows = slice(r * BLOCK, (r + 1) * BLOCK)
            n, dn = normed(
                q_in[rows, cols], dq_in[rows, cols], gain, spread_rows(r), spread_rows(8 + r)
            )
            store[rows, 0:HEAD_DIM] = dn
            store[rows, HEAD_DIM:] = n

    def q_across(x, i):
        return pltpu.make_async_remote_copy(
            q_send.at[x, pl.ds(i * QT, QT)],
            qq.at[x, pl.ds(ROWS + i * QT, QT)],
            yq_s.at[x, i],
            yq_r.at[x, i],
            device_id=across,
            device_id_type=MESH,
        )

    norm_queries(theirs(0), q_send.at[0])
    for i in range(n_q):
        q_across(0, i).start()
    arrived_across(0, 1)
    first_hop(0, 1, 1)
    norm_queries(theirs(1), q_send.at[1])
    for x in range(3):
        norm_queries(mine(x), qq.at[x, pl.ds(0, ROWS)])

    def arrive(x, d, part, typ):
        for direction in range(2):

            @pl.when(jnp.logical_or(d < last, typ == direction))
            def _():
                ring(x, part, typ, direction, d - 1).wait_recv()

            @pl.when(jnp.logical_or(d < last - 1, jnp.logical_and(d == last - 1, typ == direction)))
            def _():
                ring(x, part, typ, direction, d).start()

    def own_copy(x, i, which):
        cols = pl.ds(pl.multiple_of(jnp.where(x < 2, 2 * y + x, 4) * HEAD_DIM, HEAD_DIM), HEAD_DIM)
        rows = pl.ds(pl.multiple_of(i * QT, QT), QT)
        return pltpu.make_async_copy(
            out.at[which, x, rows],
            (oa_hbm, ot_hbm)[which].at[rows, cols],
            o_s.at[which, x, i],
        )

    def copy_across(x, i, which):
        cols = pl.ds(pl.multiple_of((2 * y + x) * HEAD_DIM, HEAD_DIM), HEAD_DIM)
        return pltpu.make_async_remote_copy(
            out.at[which, x, pl.ds(pl.multiple_of(ROWS + i * QT, QT), QT)],
            (oa_hbm, ot_hbm)[which].at[pl.ds(pl.multiple_of(i * QT, QT), QT), cols],
            o_s.at[which, x, n_q + i],
            o_r.at[which, x, i],
            device_id=across,
            device_id_type=MESH,
        )

    def attend(x, rows, first, count):
        pair = qq[x, rows, :]
        query = pair[:, HEAD_DIM:]
        contract = (((1,), (1,)), ((), ()))
        size = 2 * BLOCK * count
        keys = kv[x, 1, pl.ds(first, count)].reshape(size, 2 * HEAD_DIM)
        vals = kv[x, 0, pl.ds(first, count)].reshape(size, 2 * HEAD_DIM)
        scores = lax.dot_general(query, keys[:, :HEAD_DIM], contract, preferred_element_type=F32)
        slopes = lax.dot_general(pair, keys, contract, preferred_element_type=F32)
        top = jnp.max(scores, axis=1, keepdims=True)
        before = m_ref[x, rows, :]
        newest = jnp.maximum(before, top * (scale * LOG2E))
        factor = jnp.exp2(before - newest)
        m_ref[x, rows, :] = newest
        total_w = l_ref[x, rows, :] * factor
        total_m = sp_ref[x, rows, :] * factor
        w = jnp.exp2(scores * (scale * LOG2E) - newest[:, 0:1])
        mix = w * slopes
        for i in range(0, size, HEAD_DIM):
            total_w = total_w + w[:, i : i + HEAD_DIM]
            total_m = total_m + mix[:, i : i + HEAD_DIM]
        both = jnp.dot(w.astype(BF16), vals, preferred_element_type=F32)
        mixed = jnp.dot(mix.astype(BF16), vals[:, :HEAD_DIM], preferred_element_type=F32)
        primal = acc[x, rows, 0:HEAD_DIM] * factor + both[:, :HEAD_DIM]
        tangent = acc[x, rows, HEAD_DIM:] * factor + both[:, HEAD_DIM:] + mixed * scale
        l_ref[x, rows, :] = total_w
        sp_ref[x, rows, :] = total_m
        acc[x, rows, 0:HEAD_DIM] = primal
        acc[x, rows, HEAD_DIM:] = tangent

    def tile(x, d, t):
        rows = pl.ds(pl.multiple_of(t * QT, QT), QT)
        @pl.when(jnp.logical_and(d == 1, t >= n_q))
        def _():
            q_across(x, t - n_q).wait_recv()

        @pl.when(d == 1)
        def _():
            acc[x, rows, :] = jnp.zeros((QT, 2 * HEAD_DIM), F32)
            m_ref[x, rows, :] = jnp.full((QT, HEAD_DIM), -1e30, F32)
            l_ref[x, rows, :] = jnp.zeros((QT, HEAD_DIM), F32)
            sp_ref[x, rows, :] = jnp.zeros((QT, HEAD_DIM), F32)

        pl.when(d == 1)(lambda: attend(x, rows, 0, 3))
        pl.when(jnp.logical_and(d > 1, d < last))(lambda: attend(x, rows, 2 * d - 1, 2))
        pl.when(d == last)(lambda: attend(x, rows, n_z - 1, 1))

        @pl.when(d == last)
        def _():
            whole = jnp.sum(l_ref[x, rows, :], axis=1, keepdims=True)
            inv = 1.0 / whole
            ratio = jnp.sum(sp_ref[x, rows, :], axis=1, keepdims=True) * scale * inv
            first = acc[x, rows, 0:HEAD_DIM] * inv
            out[0, x, rows, :] = first.astype(BF16)
            out[1, x, rows, :] = (acc[x, rows, HEAD_DIM:] * inv - ratio * first).astype(BF16)

            @pl.when(t < n_q)
            def _():
                for which in range(2):
                    own_copy(x, t, which).start()

            @pl.when(t >= n_q)
            def _():
                for which in range(2):
                    copy_across(x, t - n_q, which).start()

    steps = 3 * last

    def turn(g):
        order = ORDER
        x, d = order[-1]
        for i, (xi, di) in enumerate(order[:-1]):
            x = jnp.where(g == i, xi, x)
            d = jnp.where(g == i, di, d)
        return x, d

    def step(g, carry):
        x, d = turn(g)
        xb, db = turn(jnp.maximum(g - 1, 0))
        tiles = jnp.where(g == 0, 0, jnp.where(xb == 2, n_q, 2 * n_q))

        @pl.when(g == 1)
        def _():
            for send in yv_sends[4:] + yk_sends[2:]:
                send.start()

        @pl.when(g == 2)
        def _():
            for i in range(n_q):
                q_across(1, i).start()

        def sub(i, carry):
            lax.fori_loop(
                lax.div(tiles * i + 3, 4),
                lax.div(tiles * (i + 1) + 3, 4),
                lambda t, carry: (
                    tile(xb, db, jnp.where(db == last, tiles - 1 - t, t)),
                    carry,
                )[1],
                0,
            )

            @pl.when(g < steps)
            def _():
                arrive(x, d, lax.div(i, 2), lax.rem(i, 2))

            for head, start in ((1, SECOND_STARTS), (2, THIRD_STARTS)):
                for k, (part, typ) in enumerate(((0, 1), (1, 0), (1, 1))):

                    @pl.when(jnp.logical_and(g == start, i == k))
                    def _(head=head, part=part, typ=typ):
                        if typ == 1:
                            arrived_across(head, part)
                        first_hop(head, part, typ)

            return carry

        lax.fori_loop(0, 4, sub, 0)
        return carry

    lax.fori_loop(0, steps + 1, step, 0)

    for send in stat_sends + yv_sends + yk_sends:
        send.wait_send()
    for x in range(2):
        for i in range(n_q):
            q_across(x, i).wait_send()

    def drain(i, carry):
        x, part = lax.div(i, 2), lax.rem(i, 2)
        for typ in range(2):
            for hop in range(last):
                for direction in range(2):
                    if hop < last - 1 or direction == typ:
                        ring(x, part, typ, direction, hop).wait_send()
        return carry

    lax.fori_loop(0, 6, drain, 0)

    def drain_out(i, carry):
        for which in range(2):
            for x in range(3):
                own_copy(x, i, which).wait()
                if x < 2:
                    copy_across(x, i, which).wait_send()
                    copy_across(x, i, which).wait_recv()
        return carry

    lax.fori_loop(0, n_q, drain_out, 0)


def copies(oa_src, ot_src, oa_dst, ot_dst, sem):
    moves = [
        pltpu.make_async_copy(src, dst, sem.at[j])
        for j, (src, dst) in enumerate(((oa_src, oa_dst), (ot_src, ot_dst)))
    ]
    for move in moves:
        move.start()
    for move in moves:
        move.wait()


def settle(first, second):
    anywhere = pl.BlockSpec(memory_space=pl.ANY)
    return tuple(
        pl.pallas_call(
            copies,
            out_shape=[jax.ShapeDtypeStruct(first.shape, BF16)] * 2,
            in_specs=[anywhere] * 2,
            out_specs=[anywhere] * 2,
            scratch_shapes=[pltpu.SemaphoreType.DMA((2,))],
            compiler_params=pltpu.CompilerParams(vmem_limit_bytes=4 * 2**20),
        )(first, second)
    )


def shards(mesh, queries, query_tangent, keys, key_tangent, values, value_tangent, query_gain, key_gain):
    n_head = mesh.shape["head"]
    n_z = mesh.shape["ctx"] // 2
    width = queries.shape[1]
    dma = pltpu.SemaphoreType.DMA
    anywhere = pl.BlockSpec(memory_space=pl.ANY)
    vmem = pl.BlockSpec(memory_space=pltpu.VMEM)
    n_q = ROWS // QT
    results = pl.pallas_call(
        functools.partial(kernel, width, n_head, n_z),
        out_shape=[pltpu.VMEM(queries.shape, BF16)] * 2,
        in_specs=[anywhere] * 6 + [vmem] * 2,
        out_specs=[anywhere] * 2,
        scratch_shapes=[
            pltpu.VMEM((ROWS, width), BF16),
            pltpu.VMEM((ROWS, width), BF16),
            pltpu.VMEM((BLOCK, width), BF16),
            pltpu.VMEM((BLOCK, width), BF16),
            pltpu.VMEM((n_head, 16, BLOCK), F32),
            pltpu.VMEM((16, BLOCK), F32),
            pltpu.VMEM((3, 2 * ROWS, 2 * HEAD_DIM), BF16),
            pltpu.VMEM((2, ROWS, 2 * HEAD_DIM), BF16),
            pltpu.VMEM((3, 2, n_z, 2, BLOCK, 2 * HEAD_DIM), BF16),
            pltpu.VMEM((2, BLOCK, 2 * HEAD_DIM), BF16),
            pltpu.VMEM((3, 2 * ROWS, 2 * HEAD_DIM), F32),
            pltpu.VMEM((3, 2 * ROWS, HEAD_DIM), F32),
            pltpu.VMEM((3, 2 * ROWS, HEAD_DIM), F32),
            pltpu.VMEM((3, 2 * ROWS, HEAD_DIM), F32),
            pltpu.VMEM((2, 3, 2 * ROWS, HEAD_DIM), BF16),
            dma((4,)),
            dma((3, 2)),
            dma((n_head - 1,)),
            dma((n_head,)),
            dma((3, 2)),
            dma((3, 2)),
            dma((3,)),
            dma((3,)),
            dma((2, n_q)),
            dma((2, n_q)),
            dma((2, 3, 2, 2, n_z // 2)),
            dma((3, 2, n_z, 2)),
            dma((2, 3, 2 * n_q)),
            dma((2, 2, n_q)),
        ],
        compiler_params=pltpu.CompilerParams(
            collective_id=0, has_side_effects=True, vmem_limit_bytes=58 * 2**20
        ),
        cost_estimate=pl.CostEstimate(
            flops=12 * 5 * ROWS * 16 * BLOCK * HEAD_DIM,
            bytes_accessed=5 * 2**20,
            transcendentals=5 * ROWS * 16 * BLOCK,
        ),
    )(
        queries,
        query_tangent,
        keys,
        key_tangent,
        values,
        value_tangent,
        query_gain,
        key_gain,
    )
    return settle(*results)


def solution(mesh):
    rows = P(("dp", "ctx"), "head")
    return jax.shard_map(
        functools.partial(shards, mesh),
        mesh=mesh,
        in_specs=(rows,) * 6 + (P("head"),) * 2,
        out_specs=(rows, rows),
        check_vma=False,
    )
```

```python
import functools

import jax
import jax.numpy as jnp
from jax import lax
from jax.experimental import pallas as pl
from jax.experimental.pallas import tpu as pltpu
from jax.sharding import PartitionSpec as P

HEAD_DIM = 128
MESH = pl.DeviceIdType.MESH
ROWS = 768
BLOCK = 128
QT = 768
EPS = 1e-6
ORDER = ((0, 1), (0, 2), (1, 1), (0, 3), (1, 2), (0, 4), (1, 3), (2, 1), (1, 4), (2, 2), (2, 3), (2, 4))
SECOND_STARTS, THIRD_STARTS = 0, 5
LOG2E = 1.4426950408889634
F32 = jnp.float32
BF16 = jnp.bfloat16


def kernel(
    width,
    n_head,
    n_z,
    q_hbm,
    dq_hbm,
    k_hbm,
    dk_hbm,
    v_hbm,
    dv_hbm,
    qg_ref,
    kg_ref,
    oa_hbm,
    ot_hbm,
    q_in,
    dq_in,
    k_in,
    dk_in,
    stat,
    coef,
    qq,
    q_send,
    kv,
    k_send,
    acc,
    m_ref,
    l_ref,
    sp_ref,
    out,
    in_sem,
    vl_sem,
    st_s,
    st_r,
    yv_s,
    yv_r,
    yk_s,
    yk_r,
    yq_s,
    yq_r,
    z_s,
    z_r,
    o_s,
    o_r,
):
    c = lax.axis_index("ctx")
    h = lax.axis_index("head")
    p = lax.axis_index("dp")
    z = lax.div(c, 2)
    y = lax.rem(c, 2)
    right = (2 * lax.rem(z + 1, n_z) + y, h, p)
    left = (2 * lax.rem(z + n_z - 1, n_z) + y, h, p)
    across = (2 * z + 1 - y, h, p)
    head_peers = [(c, lax.rem(h + i, n_head), p) for i in range(1, n_head)]
    scale = HEAD_DIM ** (-0.5)
    last = n_z // 2
    home = n_z - 1
    n_q = ROWS // QT
    q_blocks = ROWS // BLOCK

    def mine(x):
        return pl.multiple_of((2 * y + x if x < 2 else 4) * HEAD_DIM, HEAD_DIM)

    def theirs(x):
        return pl.multiple_of((2 * (1 - y) + x if x < 2 else 4) * HEAD_DIM, HEAD_DIM)

    v_loads = [
        pltpu.make_async_copy(
            src.at[:, pl.ds(mine(x), HEAD_DIM)],
            kv.at[x, 0, home, 0, :, pl.ds(half * HEAD_DIM, HEAD_DIM)],
            vl_sem.at[x, half],
        )
        for x in range(3)
        for half, src in enumerate((v_hbm, dv_hbm))
    ]
    for load in v_loads:
        load.start()

    loads = [
        pltpu.make_async_copy(src, dst, in_sem.at[i])
        for i, (src, dst) in enumerate(
            ((k_hbm, k_in), (dk_hbm, dk_in), (q_hbm, q_in), (dq_hbm, dq_in))
        )
    ]
    for load in loads:
        load.start()
    barrier = pltpu.get_barrier_semaphore()
    for peer in [right, left, across] + head_peers:
        pl.semaphore_signal(barrier, inc=1, device_id=peer, device_id_type=MESH)

    pl.semaphore_wait(barrier, 3 + len(head_peers))

    yv_sends = [
        pltpu.make_async_remote_copy(
            src.at[:, pl.ds(theirs(x), HEAD_DIM)],
            kv.at[x, 0, home, 1, :, pl.ds(half * HEAD_DIM, HEAD_DIM)],
            yv_s.at[x, half],
            yv_r.at[x, half],
            device_id=across,
            device_id_type=MESH,
        )
        for x in range(3)
        for half, src in enumerate((v_hbm, dv_hbm))
    ]
    for send in yv_sends[:4]:
        send.start()

    def ring(x, part, typ, direction, hop):
        src = jnp.where(hop == 0, home, 2 * (hop - 1) + direction)
        dst = jnp.minimum(2 * hop + direction, home - 1)
        return pltpu.make_async_remote_copy(
            kv.at[x, part, src, typ],
            kv.at[x, part, dst, typ],
            z_s.at[direction, x, part, typ, hop],
            z_r.at[x, part, dst, typ],
            device_id=right if direction == 0 else left,
            device_id_type=MESH,
        )

    def first_hop(x, part, typ):
        for direction in range(2):
            ring(x, part, typ, direction, 0).start()

    for x in range(3):
        v_loads[2 * x].wait()
        v_loads[2 * x + 1].wait()
        first_hop(x, 0, 0)

    def row_sums(a, b):
        field = a.astype(F32)
        tangent = b.astype(F32)
        square = field * field
        cross = field * tangent
        folded = [
            functools.reduce(
                jnp.add, [t[:, i : i + BLOCK] for i in range(0, width, BLOCK)]
            )
            for t in (square, cross)
        ]
        return [jnp.sum(t.T, axis=0, keepdims=True) for t in folded]

    loads[0].wait()
    loads[1].wait()
    sums_k = row_sums(k_in[...], dk_in[...])
    stat[h, 6:7, :] = sums_k[0]
    stat[h, 7:8, :] = jnp.zeros((1, BLOCK), F32)
    stat[h, 14:15, :] = sums_k[1]
    stat[h, 15:16, :] = jnp.zeros((1, BLOCK), F32)
    loads[2].wait()
    loads[3].wait()
    for r in range(q_blocks):
        rows = slice(r * BLOCK, (r + 1) * BLOCK)
        sums_q = row_sums(q_in[rows, :], dq_in[rows, :])
        stat[h, r : r + 1, :] = sums_q[0]
        stat[h, 8 + r : 9 + r, :] = sums_q[1]

    stat_sends = [
        pltpu.make_async_remote_copy(
            stat.at[h],
            stat.at[h],
            st_s.at[i],
            st_r.at[h],
            device_id=peer,
            device_id_type=MESH,
        )
        for i, peer in enumerate(head_peers)
    ]
    for send in stat_sends:
        send.start()

    def arrived_across(x, part):
        if part == 1:
            pltpu.make_async_remote_copy(
                kv.at[x, 1, home, 0],
                kv.at[x, 1, home, 1],
                yk_s.at[x],
                yk_r.at[x],
                device_id=across,
                device_id_type=MESH,
            ).wait_recv()
        else:
            for half, src in enumerate((v_hbm, dv_hbm)):
                pltpu.make_async_remote_copy(
                    src.at[:, pl.ds(theirs(x), HEAD_DIM)],
                    kv.at[x, 0, home, 1, :, pl.ds(half * HEAD_DIM, HEAD_DIM)],
                    yv_s.at[x, half],
                    yv_r.at[x, half],
                    device_id=across,
                    device_id_type=MESH,
                ).wait_recv()

    arrived_across(0, 0)
    first_hop(0, 0, 1)

    for i in range(1, n_head):
        sender = lax.rem(h + i, n_head)
        pltpu.make_async_remote_copy(
            stat.at[sender],
            stat.at[sender],
            st_s.at[i - 1],
            st_r.at[sender],
            device_id=head_peers[i - 1],
            device_id_type=MESH,
        ).wait_recv()
    total = functools.reduce(jnp.add, [stat[i] for i in range(n_head)])
    mean = total * (1.0 / (width * n_head))
    inverse = lax.rsqrt(mean[:8] + EPS)
    coef[0:8, :] = inverse
    coef[8:16, :] = inverse * inverse * inverse * mean[8:]

    def normed(field, tangent, gain, inv, third):
        field = field.astype(F32)
        tangent = tangent.astype(F32)
        return (
            (field * inv * gain).astype(BF16),
            (gain * (tangent * inv - field * third)).astype(BF16),
        )

    def spread_rows(row):
        return jnp.broadcast_to(coef[row : row + 1, :], (BLOCK, BLOCK)).T

    inv_k, third_k = spread_rows(6), spread_rows(14)

    def norm_keys(columns, store):
        cols = pl.ds(columns, HEAD_DIM)
        n, dn = normed(k_in[:, cols], dk_in[:, cols], kg_ref[cols].reshape(1, HEAD_DIM), inv_k, third_k)
        store[:, 0:HEAD_DIM] = n
        store[:, HEAD_DIM:] = dn

    yk_sends = [
        pltpu.make_async_remote_copy(
            k_send.at[x] if x < 2 else kv.at[x, 1, home, 0],
            kv.at[x, 1, home, 1],
            yk_s.at[x],
            yk_r.at[x],
            device_id=across,
            device_id_type=MESH,
        )
        for x in range(3)
    ]
    for x in range(2):
        norm_keys(theirs(x), k_send.at[x])
        yk_sends[x].start()
        norm_keys(mine(x), kv.at[x, 1, home, 0])
        if x == 0:
            first_hop(0, 1, 0)
    norm_keys(mine(2), kv.at[2, 1, home, 0])

    def norm_queries(columns, store):
        cols = pl.ds(columns, HEAD_DIM)
        gain = qg_ref[cols].reshape(1, HEAD_DIM)
        for r in range(q_blocks):
            rows = slice(r * BLOCK, (r + 1) * BLOCK)
            n, dn = normed(
                q_in[rows, cols], dq_in[rows, cols], gain, spread_rows(r), spread_rows(8 + r)
            )
            store[rows, 0:HEAD_DIM] = dn
            store[rows, HEAD_DIM:] = n

    def q_across(x, i):
        return pltpu.make_async_remote_copy(
            q_send.at[x, pl.ds(i * QT, QT)],
            qq.at[x, pl.ds(ROWS + i * QT, QT)],
            yq_s.at[x, i],
            yq_r.at[x, i],
            device_id=across,
            device_id_type=MESH,
        )

    norm_queries(theirs(0), q_send.at[0])
    for i in range(n_q):
        q_across(0, i).start()
    arrived_across(0, 1)
    first_hop(0, 1, 1)
    norm_queries(mine(0), qq.at[0, pl.ds(0, ROWS)])

    def arrive(x, d, part, typ):
        for direction in range(2):

            @pl.when(jnp.logical_or(d < last, typ == direction))
            def _():
                ring(x, part, typ, direction, d - 1).wait_recv()

            @pl.when(jnp.logical_or(d < last - 1, jnp.logical_and(d == last - 1, typ == direction)))
            def _():
                ring(x, part, typ, direction, d).start()

    def own_copy(x, i, which):
        cols = pl.ds(pl.multiple_of(jnp.where(x < 2, 2 * y + x, 4) * HEAD_DIM, HEAD_DIM), HEAD_DIM)
        rows = pl.ds(pl.multiple_of(i * QT, QT), QT)
        return pltpu.make_async_copy(
            out.at[which, x, rows],
            (oa_hbm, ot_hbm)[which].at[rows, cols],
            o_s.at[which, x, i],
        )

    def copy_across(x, i, which):
        cols = pl.ds(pl.multiple_of((2 * y + x) * HEAD_DIM, HEAD_DIM), HEAD_DIM)
        return pltpu.make_async_remote_copy(
            out.at[which, x, pl.ds(pl.multiple_of(ROWS + i * QT, QT), QT)],
            (oa_hbm, ot_hbm)[which].at[pl.ds(pl.multiple_of(i * QT, QT), QT), cols],
            o_s.at[which, x, n_q + i],
            o_r.at[which, x, i],
            device_id=across,
            device_id_type=MESH,
        )

    def tile(x, d, t):
        rows = pl.ds(pl.multiple_of(t * QT, QT), QT)
        @pl.when(jnp.logical_and(d == 1, t >= n_q))
        def _():
            q_across(x, t - n_q).wait_recv()

        @pl.when(d == 1)
        def _():
            acc[x, rows, :] = jnp.zeros((QT, 2 * HEAD_DIM), F32)
            m_ref[x, rows, :] = jnp.full((QT, HEAD_DIM), -1e30, F32)
            l_ref[x, rows, :] = jnp.zeros((QT, HEAD_DIM), F32)
            sp_ref[x, rows, :] = jnp.zeros((QT, HEAD_DIM), F32)

        pair = qq[x, rows, :]
        query = pair[:, HEAD_DIM:]
        contract = (((1,), (1,)), ((), ()))
        keys = kv[x, 1, pl.ds(2 * (d - 1), 2)].reshape(4 * BLOCK, 2 * HEAD_DIM)
        vals = kv[x, 0, pl.ds(2 * (d - 1), 2)].reshape(4 * BLOCK, 2 * HEAD_DIM)
        scores = lax.dot_general(query, keys[:, :HEAD_DIM], contract, preferred_element_type=F32)
        slopes = lax.dot_general(pair, keys, contract, preferred_element_type=F32)
        top = jnp.max(scores, axis=1, keepdims=True)
        before = m_ref[x, rows, :]
        newest = jnp.maximum(before, top * (scale * LOG2E))
        factor = jnp.exp2(before - newest)
        m_ref[x, rows, :] = newest
        total_w = l_ref[x, rows, :] * factor
        total_m = sp_ref[x, rows, :] * factor
        w = jnp.exp2(scores * (scale * LOG2E) - newest[:, 0:1])
        mix = w * slopes
        for i in range(0, 4 * BLOCK, HEAD_DIM):
            total_w = total_w + w[:, i : i + HEAD_DIM]
            total_m = total_m + mix[:, i : i + HEAD_DIM]
        both = jnp.dot(w.astype(BF16), vals, preferred_element_type=F32)
        mixed = jnp.dot(mix.astype(BF16), vals[:, :HEAD_DIM], preferred_element_type=F32)
        primal = acc[x, rows, 0:HEAD_DIM] * factor + both[:, :HEAD_DIM]
        tangent = acc[x, rows, HEAD_DIM:] * factor + both[:, HEAD_DIM:] + mixed * scale
        l_ref[x, rows, :] = total_w
        sp_ref[x, rows, :] = total_m
        acc[x, rows, 0:HEAD_DIM] = primal
        acc[x, rows, HEAD_DIM:] = tangent

        @pl.when(d == last)
        def _():
            whole = jnp.sum(l_ref[x, rows, :], axis=1, keepdims=True)
            inv = 1.0 / whole
            ratio = jnp.sum(sp_ref[x, rows, :], axis=1, keepdims=True) * scale * inv
            first = acc[x, rows, 0:HEAD_DIM] * inv
            out[0, x, rows, :] = first.astype(BF16)
            out[1, x, rows, :] = (acc[x, rows, HEAD_DIM:] * inv - ratio * first).astype(BF16)

            @pl.when(t < n_q)
            def _():
                for which in range(2):
                    own_copy(x, t, which).start()

            @pl.when(t >= n_q)
            def _():
                for which in range(2):
                    copy_across(x, t - n_q, which).start()

    steps = 3 * last

    def turn(g):
        order = ORDER
        x, d = order[-1]
        for i, (xi, di) in enumerate(order[:-1]):
            x = jnp.where(g == i, xi, x)
            d = jnp.where(g == i, di, d)
        return x, d

    def step(g, carry):
        x, d = turn(g)
        xb, db = turn(jnp.maximum(g - 1, 0))
        tiles = jnp.where(g == 0, 0, jnp.where(xb == 2, n_q, 2 * n_q))

        @pl.when(g == 1)
        def _():
            for send in yv_sends[4:] + yk_sends[2:]:
                send.start()

        @pl.when(g == 2)
        def _():
            norm_queries(theirs(1), q_send.at[1])
            for i in range(n_q):
                q_across(1, i).start()
            norm_queries(mine(1), qq.at[1, pl.ds(0, ROWS)])

        @pl.when(g == 4)
        def _():
            norm_queries(mine(2), qq.at[2, pl.ds(0, ROWS)])

        def sub(i, carry):
            lax.fori_loop(
                lax.div(tiles * i + 3, 4),
                lax.div(tiles * (i + 1) + 3, 4),
                lambda t, carry: (
                    tile(xb, db, jnp.where(db == last, tiles - 1 - t, t)),
                    carry,
                )[1],
                0,
            )

            @pl.when(g < steps)
            def _():
                arrive(x, d, lax.div(i, 2), lax.rem(i, 2))

            for head, start in ((1, SECOND_STARTS), (2, THIRD_STARTS)):
                for k, (part, typ) in enumerate(((0, 1), (1, 0), (1, 1))):

                    @pl.when(jnp.logical_and(g == start, i == k))
                    def _(head=head, part=part, typ=typ):
                        if typ == 1:
                            arrived_across(head, part)
                        first_hop(head, part, typ)

            return carry

        lax.fori_loop(0, 4, sub, 0)
        return carry

    lax.fori_loop(0, steps + 1, step, 0)

    for send in stat_sends + yv_sends + yk_sends:
        send.wait_send()
    for x in range(2):
        for i in range(n_q):
            q_across(x, i).wait_send()

    def drain(i, carry):
        x, part = lax.div(i, 2), lax.rem(i, 2)
        for typ in range(2):
            for hop in range(last):
                for direction in range(2):
                    if hop < last - 1 or direction == typ:
                        ring(x, part, typ, direction, hop).wait_send()
        return carry

    lax.fori_loop(0, 6, drain, 0)

    def drain_out(i, carry):
        for which in range(2):
            for x in range(3):
                own_copy(x, i, which).wait()
                if x < 2:
                    copy_across(x, i, which).wait_send()
                    copy_across(x, i, which).wait_recv()
        return carry

    lax.fori_loop(0, n_q, drain_out, 0)


def copies(oa_src, ot_src, oa_dst, ot_dst, sem):
    moves = [
        pltpu.make_async_copy(src, dst, sem.at[j])
        for j, (src, dst) in enumerate(((oa_src, oa_dst), (ot_src, ot_dst)))
    ]
    for move in moves:
        move.start()
    for move in moves:
        move.wait()


def settle(first, second):
    anywhere = pl.BlockSpec(memory_space=pl.ANY)
    return tuple(
        pl.pallas_call(
            copies,
            out_shape=[jax.ShapeDtypeStruct(first.shape, BF16)] * 2,
            in_specs=[anywhere] * 2,
            out_specs=[anywhere] * 2,
            scratch_shapes=[pltpu.SemaphoreType.DMA((2,))],
            compiler_params=pltpu.CompilerParams(vmem_limit_bytes=4 * 2**20),
        )(first, second)
    )


def shards(mesh, queries, query_tangent, keys, key_tangent, values, value_tangent, query_gain, key_gain):
    n_head = mesh.shape["head"]
    n_z = mesh.shape["ctx"] // 2
    width = queries.shape[1]
    dma = pltpu.SemaphoreType.DMA
    anywhere = pl.BlockSpec(memory_space=pl.ANY)
    vmem = pl.BlockSpec(memory_space=pltpu.VMEM)
    n_q = ROWS // QT
    results = pl.pallas_call(
        functools.partial(kernel, width, n_head, n_z),
        out_shape=[pltpu.VMEM(queries.shape, BF16)] * 2,
        in_specs=[anywhere] * 6 + [vmem] * 2,
        out_specs=[anywhere] * 2,
        scratch_shapes=[
            pltpu.VMEM((ROWS, width), BF16),
            pltpu.VMEM((ROWS, width), BF16),
            pltpu.VMEM((BLOCK, width), BF16),
            pltpu.VMEM((BLOCK, width), BF16),
            pltpu.VMEM((n_head, 16, BLOCK), F32),
            pltpu.VMEM((16, BLOCK), F32),
            pltpu.VMEM((3, 2 * ROWS, 2 * HEAD_DIM), BF16),
            pltpu.VMEM((2, ROWS, 2 * HEAD_DIM), BF16),
            pltpu.VMEM((3, 2, n_z, 2, BLOCK, 2 * HEAD_DIM), BF16),
            pltpu.VMEM((2, BLOCK, 2 * HEAD_DIM), BF16),
            pltpu.VMEM((3, 2 * ROWS, 2 * HEAD_DIM), F32),
            pltpu.VMEM((3, 2 * ROWS, HEAD_DIM), F32),
            pltpu.VMEM((3, 2 * ROWS, HEAD_DIM), F32),
            pltpu.VMEM((3, 2 * ROWS, HEAD_DIM), F32),
            pltpu.VMEM((2, 3, 2 * ROWS, HEAD_DIM), BF16),
            dma((4,)),
            dma((3, 2)),
            dma((n_head - 1,)),
            dma((n_head,)),
            dma((3, 2)),
            dma((3, 2)),
            dma((3,)),
            dma((3,)),
            dma((2, n_q)),
            dma((2, n_q)),
            dma((2, 3, 2, 2, n_z // 2)),
            dma((3, 2, n_z, 2)),
            dma((2, 3, 2 * n_q)),
            dma((2, 2, n_q)),
        ],
        compiler_params=pltpu.CompilerParams(
            collective_id=0, has_side_effects=True, vmem_limit_bytes=58 * 2**20
        ),
        cost_estimate=pl.CostEstimate(
            flops=12 * 5 * ROWS * 16 * BLOCK * HEAD_DIM,
            bytes_accessed=5 * 2**20,
            transcendentals=5 * ROWS * 16 * BLOCK,
        ),
    )(
        queries,
        query_tangent,
        keys,
        key_tangent,
        values,
        value_tangent,
        query_gain,
        key_gain,
    )
    return settle(*results)


def solution(mesh):
    rows = P(("dp", "ctx"), "head")
    return jax.shard_map(
        functools.partial(shards, mesh),
        mesh=mesh,
        in_specs=(rows,) * 6 + (P("head"),) * 2,
        out_specs=(rows, rows),
        check_vma=False,
    )
```
